128 devices in a mesh: col: 32 (over z, x, y_hi), row: 4 (over y_lo, core).
Axes of the slice: x: 4, y: 4 (y_hi: 2, y_lo: 2; y = y_hi * 2 + y_lo), z: 4, core: 2. Of those that a mesh axis runs over, the one named last changes fastest.
Arguments:
- inverse_block: float32 [8192, 8192], P('row', 'col'), may hold values from -6 to 6
- panels: float32 [64, 2048, 256], P('col', 'row'), may hold values from -0.125 to 0.125
- pattern: int32 [64, 8], replicated, may hold values from 0 to 31, as said below
- active: int32 [64], replicated, may hold values 0 or 1
Outputs:
- selected: float32 [16384, 8192], P('row', 'col')
The draws below stay inside these ranges and needn't reach their ends.
Inputs may be any that keep to these rules, and one draw needn't show every extreme that they name: `pattern`: within each row, the entries g * 2 to (g + 1) * 2 - 1 are distinct and lie in g * 8 to (g + 1) * 8 - 1, for each group g of 2 consecutive entries.
All inputs are finite; a program needn't handle non-finite values.
Results may differ from the reference program's by a relative error of at most 0.0003.
Values sent between devices are 32-bit elements; how exact they have to be, the bound alone decides.
A program may use at most 256 MiB of HBM per device.

```python
import jax
import jax.numpy as jnp
from jax import lax

B = 256
MR = 2
KT = 64
NA = 32
M = 8
N_ROW = 4


def draw_pattern(key, part):
    key = jax.random.fold_in(key, 7)
    rows_local = NA // N_ROW
    ordered = jnp.broadcast_to(jnp.arange(rows_local, dtype=jnp.int32), (KT * N_ROW, rows_local))
    shuffled = jax.random.permutation(key, ordered, axis=1, independent=True)
    picked = shuffled[:, :MR].reshape(KT, N_ROW, MR)
    group_start = jnp.arange(N_ROW, dtype=jnp.int32)[None, :, None] * rows_local
    return (picked + group_start).reshape(KT, M)


def place_ends(result, own_key, least, top_value):
    extent = result.shape
    spot = [jax.random.randint(jax.random.fold_in(own_key, axis), (), 0, extent[axis]) for axis in range(len(extent))]
    result = result.at[tuple(spot)].set(least)
    longest = extent.index(max(extent))
    spot[longest] = (spot[longest] + 1) % extent[longest]
    return result.at[tuple(spot)].set(top_value)


def steps_of(rng, extent, pieces, low, high):
    gain, own = 1.0, jax.random.fold_in(rng, 6)
    for axis_at, blocks in pieces:
        heights = jnp.exp(jax.random.uniform(jax.random.fold_in(own, axis_at), (blocks,), jnp.float32, low / len(pieces), high / len(pieces)))
        gain = gain * jnp.repeat(heights, extent[axis_at] // blocks).reshape([-1 if axis == axis_at else 1 for axis in range(len(extent))])
    return gain


def scatter_about(own_key, dims, scale, limit, pieces=(), kind=jnp.bfloat16):
    result = scale * jax.random.normal(own_key, dims, jnp.float32)
    if pieces:
        result = result * steps_of(own_key, dims, pieces, -0.22, 0.18)
    return jnp.clip(result, -limit, limit).astype(kind)


def setup_inputs(seed: int = 0) -> dict:
    arg_keys = jax.random.split(jax.random.key(seed), 5)
    return {
        "inverse_block": scatter_about(arg_keys[0], (NA * B, NA * B), 1.0, 6.0, ((0, 4), (1, 32)), jnp.float32),
        "panels": scatter_about(arg_keys[1], (KT, M * B, B), (M * B) ** -0.5, 0.125, ((0, 32), (1, 4)), jnp.float32),
        "pattern": draw_pattern(jax.random.fold_in(arg_keys[4], 71), 0),
        "active": place_ends((jax.random.randint(arg_keys[3], (KT,), 0, 3) < 2).astype(jnp.int32), jax.random.fold_in(arg_keys[3], 1), 0, 1),
    }


def reference(inverse_block, panels, pattern, active):
    blocks = inverse_block.reshape(NA, B, NA * B)

    def one_slot(items):
        panel, rows_used, flag = items
        chosen = jnp.take(blocks, rows_used.astype(jnp.int32), axis=0)
        product = jnp.einsum("mab,mac->bc", panel.reshape(M, B, B), chosen, precision=lax.Precision.HIGHEST)
        return -flag.astype(jnp.float32) * product

    stacked = lax.map(one_slot, (panels, pattern, active))
    return stacked.reshape(KT * B, NA * B)
```

```python
import functools

import jax
import jax.numpy as jnp
from jax import lax
from jax.experimental import pallas as pl
from jax.experimental.pallas import tpu as pltpu
from jax.sharding import PartitionSpec as P

MESH = pl.DeviceIdType.MESH
AXIS = 4


def split(value):
    high = value.astype(jnp.bfloat16)
    low = (value - high.astype(jnp.float32)).astype(jnp.bfloat16)
    return high, low


def kernel(
    inverse_in, panels_in, pattern, active, out,
    inverse, inv_high, inv_low, pan, give, take, mine,
    own_sem, inv_send, inv_recv, pan_send, pan_recv, core_send, core_recv, out_send, out_recv, out_local,
):
    tile = panels_in.shape[2]
    depth = panels_in.shape[1]
    rows_local = inverse_in.shape[0]

    col, row = lax.axis_index("col"), lax.axis_index("row")
    z, x, y_hi = col // (2 * AXIS), col // 2 % AXIS, col % 2
    y_lo, core = row // 2, row % 2
    y = y_hi * 2 + y_lo

    def device(x_at, y_at, z_at, core_at):
        return (z_at * 2 * AXIS + x_at * 2 + y_at // 2, y_at % 2 * 2 + core_at)

    def turn(at, by):
        return (at + by + AXIS) % AXIS

    def along(axis, by):
        if axis == "x":
            return device(turn(x, by), y, z, core)
        if axis == "y":
            return device(x, turn(y, by), z, core)
        return device(x, y, turn(z, by), core)

    partner = device(x, y_hi * 2 + 1 - y_lo, z, core)
    sibling = device(x, y, z, 1 - core)

    barrier = pltpu.get_barrier_semaphore()
    peers = [along("x", 1), along("x", -1), along("z", 1), along("z", -1)]
    peers += [along("y", 1), along("y", -1), along("y", 2), sibling]
    for peer in peers:
        pl.semaphore_signal(barrier, inc=1, device_id=peer, device_id_type=MESH)
    pl.semaphore_wait(barrier, len(peers))

    sent = []
    numbers = {"inv": 0, "pan": 0}

    def push(kind, source, target, to):
        sends, receives = (inv_send, inv_recv) if kind == "inv" else (pan_send, pan_recv)
        number = numbers[kind]
        numbers[kind] += 1
        copy = pltpu.make_async_remote_copy(
            src_ref=source, dst_ref=target, send_sem=sends.at[number], recv_sem=receives.at[number],
            device_id=to, device_id_type=MESH,
        )
        copy.start()
        sent.append(copy)
        return copy

    def home(first, by_first, by_second):
        if first == "x":
            return turn(x, by_first), turn(z, by_second)
        return turn(x, by_second), turn(z, by_first)

    def piece(at, group, half=None):
        view = pan.at[at[0], at[1], group]
        if half is not None:
            view = view.at[pl.ds(half * (depth // 2), depth // 2)]
        return view

    def spread(group, at, axis, source=None):
        target = piece(at, group)
        source = target if source is None else source
        return push("pan", source, target, along(axis, 1)), push("pan", source, target, along(axis, -1))

    def relay(group, below, above, axis, arrivals):
        arrivals[0].wait_recv()
        up = push("pan", piece(below, group, 0), piece(below, group, 0), along(axis, 1))
        arrivals[1].wait_recv()
        down = push("pan", piece(above, group, 1), piece(above, group, 1), along(axis, -1))
        return up, down

    own_home = (x, z)
    other = 1 - y_lo

    swap = push("pan", panels_in.at[other], piece(own_home, y_lo), partner)

    half_rows = rows_local // 2

    def inverse_half(at, half):
        return inverse.at[at, pl.ds(half * half_rows, half_rows)]

    def own_half(half):
        return inverse_in.at[pl.ds(half * half_rows, half_rows)]

    up_0 = push("inv", own_half(0), inverse_half(y, 0), along("y", 1))
    down_1 = push("inv", own_half(1), inverse_half(y, 1), along("y", -1))
    up_1 = push("inv", own_half(1), inverse_half(y, 1), along("y", 1))
    down_0 = push("inv", own_half(0), inverse_half(y, 0), along("y", -1))

    own_panel = panels_in.at[y_lo]
    a_first = spread(y_lo, own_home, "x", own_panel)
    a_second = {0: spread(y_lo, own_home, "z", own_panel)}

    own_inverse = pltpu.make_async_copy(inverse_in, inverse.at[y], own_sem.at[0])
    own_inverse.start()
    own_pan = pltpu.make_async_copy(own_panel, piece(own_home, y_lo), own_sem.at[1])
    own_pan.start()
    own_inverse.wait()
    own_pan.wait()

    def split_inverse(at, half):
        def body(i):
            block = half * half_rows + i
            high, low = split(inverse[at, block])
            inv_high[at, block] = high
            inv_low[at, block] = low

        pl.loop(0, half_rows)(body)

    split_inverse(y, 0)
    split_inverse(y, 1)

    a_far = relay(y_lo, home("x", -1, 0), home("x", 1, 0), "x", a_first)
    a_second[-1] = spread(y_lo, home("x", -1, 0), "z")
    a_second[1] = spread(y_lo, home("x", 1, 0), "z")
    swap.wait_recv()
    b_first = spread(other, own_home, "z")
    b_second = {0: spread(other, own_home, "x")}
    a_relays = [relay(y_lo, home("x", 0, -1), home("x", 0, 1), "z", a_second[0])]
    for copy in a_far:
        copy.wait_recv()
    a_second[2] = spread(y_lo, home("x", 2, 0), "z")
    b_far = relay(other, home("z", -1, 0), home("z", 1, 0), "z", b_first)
    b_second[-1] = spread(other, home("z", -1, 0), "x")
    b_second[1] = spread(other, home("z", 1, 0), "x")
    b_relays = [relay(other, home("z", 0, -1), home("z", 0, 1), "x", b_second[0])]

    up_0.wait_recv()
    far_0 = push("inv", inverse_half(turn(y, -1), 0), inverse_half(turn(y, -1), 0), along("y", 1))
    down_1.wait_recv()
    far_1 = push("inv", inverse_half(turn(y, 1), 1), inverse_half(turn(y, 1), 1), along("y", -1))
    split_inverse(turn(y, -1), 0)
    split_inverse(turn(y, 1), 1)

    for copy in b_far:
        copy.wait_recv()
    b_second[2] = spread(other, home("z", 2, 0), "x")
    up_1.wait_recv()
    split_inverse(turn(y, -1), 1)
    down_0.wait_recv()
    split_inverse(turn(y, 1), 0)

    for by in (-1, 1, 2):
        a_relays.append(relay(y_lo, home("x", by, -1), home("x", by, 1), "z", a_second[by]))
        b_relays.append(relay(other, home("z", by, -1), home("z", by, 1), "x", b_second[by]))

    far_0.wait_recv()
    split_inverse(turn(y, 2), 0)
    far_1.wait_recv()
    split_inverse(turn(y, 2), 1)
    for pair in a_relays + b_relays:
        for copy in pair:
            copy.wait_recv()

    def multiply(x_at, z_at, total, index):
        slot = z_at * (AXIS * AXIS) + x_at * AXIS + y
        for group in range(2):
            for entry in range(2):
                owner = group * 2 + core
                block = lax.rem(pattern[slot, owner * 2 + entry], rows_local)
                high, low = split(pan[x_at, z_at, group, pl.ds(entry * tile, tile), :].T)
                for side in range(2):
                    from_high = inv_high[side * 2 + group, block]
                    from_low = inv_low[side * 2 + group, block]
                    value = jnp.dot(high, from_high, preferred_element_type=jnp.float32)
                    value += jnp.dot(low, from_high, preferred_element_type=jnp.float32)
                    value += jnp.dot(high, from_low, preferred_element_type=jnp.float32)
                    if group == 0 and entry == 0:
                        total[index, side] = value
                    else:
                        total[index, side] += value

    def places(step):
        quarter = step % 4
        x_at = turn(x, quarter + quarter // 2 * (5 - 2 * quarter))
        z_mine = turn(z, (z + core) % 2 + step // 4 * 2)
        z_other = turn(z, (z + core + 1) % 2 + step // 4 * 2)
        return x_at, z_mine, z_other

    def across(step):
        return pltpu.make_async_remote_copy(
            src_ref=give.at[step], dst_ref=take.at[step], send_sem=core_send.at[step], recv_sem=core_recv.at[step],
            device_id=sibling, device_id_type=MESH,
        )

    def out_rows(x_at, y_at):
        return out.at[pl.ds(pl.multiple_of((x_at * AXIS + y_at) * tile, tile), tile)]

    def deliver(step, x_at, side, owner_lo, to_y):
        return pltpu.make_async_remote_copy(
            src_ref=mine.at[step, side], dst_ref=out_rows(x_at, y),
            send_sem=out_send.at[step, side], recv_sem=out_recv.at[y, x_at],
            device_id=device(x, to_y, z, core), device_id_type=MESH,
        )

    def keep(step, x_at):
        return pltpu.make_async_copy(mine.at[step, y_hi], out_rows(x_at, y), out_local.at[x_at])

    def finish(step):
        x_at, z_at, _ = places(step)
        slot = z_at * (AXIS * AXIS) + x_at * AXIS + y
        factor = -active[slot].astype(jnp.float32)
        across(step).wait_recv()
        mine[step] = (mine[step] + take[step]) * factor
        owner_lo = z_at // 2
        deliver(step, x_at, 1 - y_hi, owner_lo, (1 - y_hi) * 2 + owner_lo).start()

        @pl.when(owner_lo == y_lo)
        def _():
            keep(step, x_at).start()

        @pl.when(owner_lo != y_lo)
        def _():
            deliver(step, x_at, y_hi, owner_lo, y_hi * 2 + owner_lo).start()

    def step_body(step):
        x_at, z_mine, z_other = places(step)
        multiply(x_at, z_other, give, step)
        across(step).start()
        multiply(x_at, z_mine, mine, step)

        @pl.when(step > 0)
        def _():
            finish(step - 1)

    steps = give.shape[0]
    pl.loop(0, steps)(step_body)
    finish(steps - 1)

    def settle(step):
        x_at, z_at, _ = places(step)
        owner_lo = z_at // 2
        across(step).wait_send()
        deliver(step, x_at, 1 - y_hi, owner_lo, (1 - y_hi) * 2 + owner_lo).wait_send()

        @pl.when(owner_lo == y_lo)
        def _():
            keep(step, x_at).wait()

        @pl.when(owner_lo != y_lo)
        def _():
            deliver(step, x_at, y_hi, owner_lo, y_hi * 2 + owner_lo).wait_send()

    pl.loop(0, steps)(settle)
    for copy in sent:
        copy.wait_send()
    for by in range(1, AXIS):
        for x_at in range(AXIS):
            y_at = turn(y, by)
            pltpu.make_async_remote_copy(
                src_ref=mine.at[0, 0], dst_ref=out_rows(x_at, y_at),
                send_sem=out_send.at[0, 0], recv_sem=out_recv.at[y_at, x_at],
                device_id=along("y", by), device_id_type=MESH,
            ).wait_recv()


def on_device(inverse_block, panels, pattern, active):
    rows, tile = inverse_block.shape
    rows_local = rows // tile
    depth = panels.shape[1]
    steps = AXIS * AXIS // 2
    dma = pltpu.SemaphoreType.DMA
    return pl.pallas_call(
        kernel,
        out_shape=jax.ShapeDtypeStruct((AXIS * AXIS * tile, tile), jnp.float32),
        in_specs=[pl.BlockSpec(memory_space=pl.ANY)] * 2 + [pl.BlockSpec(memory_space=pltpu.SMEM)] * 2,
        out_specs=pl.BlockSpec(memory_space=pl.ANY),
        scratch_shapes=[
            pltpu.VMEM((AXIS, rows_local, tile, tile), jnp.float32),
            pltpu.VMEM((AXIS, rows_local, tile, tile), jnp.bfloat16),
            pltpu.VMEM((AXIS, rows_local, tile, tile), jnp.bfloat16),
            pltpu.VMEM((AXIS, AXIS, 2, depth, tile), jnp.float32),
            pltpu.VMEM((steps, 2, tile, tile), jnp.float32),
            pltpu.VMEM((steps, 2, tile, tile), jnp.float32),
            pltpu.VMEM((steps, 2, tile, tile), jnp.float32),
            dma((2,)),
            dma((6,)), dma((6,)),
            dma((41,)), dma((41,)),
            dma((steps,)), dma((steps,)),
            dma((steps, 2)), dma((AXIS, AXIS)), dma((AXIS,)),
        ],
        compiler_params=pltpu.CompilerParams(
            collective_id=0, has_side_effects=True, vmem_limit_bytes=56 * 1024 * 1024
        ),
        cost_estimate=pl.CostEstimate(flops=6 * 128 * tile**3, bytes_accessed=20 * 1024 * 1024, transcendentals=0),
        name="selected_inverse",
    )(inverse_block.reshape(rows_local, tile, tile), panels, pattern, active)


def solution(mesh):
    in_specs = (P("row", "col"), P("col", "row", None), P(), P())
    out_specs = P("row", "col")
    return jax.shard_map(
        on_device, mesh=mesh, in_specs=in_specs, out_specs=out_specs, check_vma=False
    )
```

```python
import functools

import jax
import jax.numpy as jnp
from jax import lax
from jax.experimental import pallas as pl
from jax.experimental.pallas import tpu as pltpu
from jax.sharding import PartitionSpec as P

MESH = pl.DeviceIdType.MESH
AXIS = 4


def split(value):
    high = value.astype(jnp.bfloat16)
    low = (value - high.astype(jnp.float32)).astype(jnp.bfloat16)
    return high, low


def kernel(
    inverse_in, panels_in, pattern, active, out,
    inverse, inv_high, inv_low, pan, give, take, mine,
    own_sem, inv_send, inv_recv, pan_send, pan_recv, core_send, core_recv, out_send, out_recv, out_local,
):
    tile = panels_in.shape[3]
    rows_local = inverse_in.shape[0]

    col, row = lax.axis_index("col"), lax.axis_index("row")
    z, x, y_hi = col // (2 * AXIS), col // 2 % AXIS, col % 2
    y_lo, core = row // 2, row % 2
    y = y_hi * 2 + y_lo

    def device(x_at, y_at, z_at, core_at):
        return (z_at * 2 * AXIS + x_at * 2 + y_at // 2, y_at % 2 * 2 + core_at)

    def turn(at, by):
        return (at + by + AXIS) % AXIS

    def along(axis, by):
        if axis == "x":
            return device(turn(x, by), y, z, core)
        if axis == "y":
            return device(x, turn(y, by), z, core)
        return device(x, y, turn(z, by), core)

    partner = device(x, y_hi * 2 + 1 - y_lo, z, core)
    sibling = device(x, y, z, 1 - core)

    barrier = pltpu.get_barrier_semaphore()
    peers = [along("x", 1), along("x", -1), along("z", 1), along("z", -1)]
    peers += [along("y", 1), along("y", -1), along("y", 2), sibling]
    for peer in peers:
        pl.semaphore_signal(barrier, inc=1, device_id=peer, device_id_type=MESH)
    pl.semaphore_wait(barrier, len(peers))

    sent = []

    def push(kind, source, target, to):
        sends, receives = (inv_send, inv_recv) if kind == "inv" else (pan_send, pan_recv)
        number = len([held for held in sent if held[0] == kind])
        copy = pltpu.make_async_remote_copy(
            src_ref=source, dst_ref=target, send_sem=sends.at[number], recv_sem=receives.at[number],
            device_id=to, device_id_type=MESH,
        )
        copy.start()
        sent.append((kind, copy))
        return copy

    class Way:
        def __init__(self, group, entry, first, second):
            self.group, self.entry, self.first, self.second = group, entry, first, second
            self.flying = {}

        def view(self, by_first, by_second, half=None):
            by_x, by_z = (by_first, by_second) if self.first == "x" else (by_second, by_first)
            tile_at = pan.at[turn(x, by_x), turn(z, by_z), self.group, self.entry]
            return tile_at if half is None else tile_at.at[pl.ds(half * (tile // 2), tile // 2)]

        def spread(self, key, axis, at, source=None):
            source = self.view(*at) if source is None else source
            self.flying[key] = [push("pan", source, self.view(*at), along(axis, by)) for by in (1, -1)]

        def relay(self, key, axis, at_below, at_above):
            up, down = self.flying[key]
            up.wait_recv()
            below = self.view(*at_below, half=0)
            far_up = push("pan", below, below, along(axis, 1))
            down.wait_recv()
            above = self.view(*at_above, half=1)
            far_down = push("pan", above, above, along(axis, -1))
            self.flying[key] = [far_up, far_down]

        def settle(self, key):
            for copy in self.flying.pop(key):
                copy.wait_recv()

        def start(self, source=None):
            self.spread("first", self.first, (0, 0), source)

        def pass_on(self):
            self.relay("first", self.first, (-1, 0), (1, 0))

        def passed(self):
            self.settle("first")

        def turn_off(self, by, source=None):
            self.spread(by, self.second, (by, 0), source)

        def turned_on(self, by):
            self.relay(by, self.second, (by, -1), (by, 1))

        def arrived(self, by):
            self.settle(by)

    other = 1 - y_lo
    near = [Way(y_lo, 0, "x", "z"), Way(y_lo, 1, "z", "x")]
    pair = [Way(other, 0, "x", "z"), Way(other, 1, "z", "x")]
    both = near + pair

    swap = push("pan", panels_in.at[other], pan.at[x, z, y_lo], partner)

    half_rows = rows_local // 2

    def inverse_half(at, half):
        return inverse.at[at, pl.ds(half * half_rows, half_rows)]

    def own_half(half):
        return inverse_in.at[pl.ds(half * half_rows, half_rows)]

    up_0 = push("inv", own_half(0), inverse_half(y, 0), along("y", 1))
    down_1 = push("inv", own_half(1), inverse_half(y, 1), along("y", -1))
    up_1 = push("inv", own_half(1), inverse_half(y, 1), along("y", 1))
    down_0 = push("inv", own_half(0), inverse_half(y, 0), along("y", -1))

    for entry, way in enumerate(near):
        way.start(panels_in.at[y_lo, entry])
    for entry, way in enumerate(near):
        way.turn_off(0, panels_in.at[y_lo, entry])

    own_inverse = pltpu.make_async_copy(inverse_in, inverse.at[y], own_sem.at[0])
    own_inverse.start()
    own_pan = pltpu.make_async_copy(panels_in.at[y_lo], pan.at[x, z, y_lo], own_sem.at[1])
    own_pan.start()
    own_inverse.wait()
    own_pan.wait()

    def split_inverse(at, half):
        def body(i):
            block = half * half_rows + i
            high, low = split(inverse[at, block])
            inv_high[at, block] = high
            inv_low[at, block] = low

        pl.loop(0, half_rows)(body)

    def multiply(x_at, z_at, total, step, side):
        slot = z_at * (AXIS * AXIS) + x_at * AXIS + y
        column = (y_hi + side) % 2
        for group in range(2):
            for entry in range(2):
                block = lax.rem(pattern[(group * 2 + core) * 2 + entry, slot], rows_local)
                high, low = split(pan[x_at, z_at, group, entry].T)
                from_high = inv_high[column * 2 + group, block]
                from_low = inv_low[column * 2 + group, block]
                value = jnp.dot(high, from_high, preferred_element_type=jnp.float32)
                value += jnp.dot(low, from_high, preferred_element_type=jnp.float32)
                value += jnp.dot(high, from_low, preferred_element_type=jnp.float32)
                if group == 0 and entry == 0:
                    total[step, side] = value
                else:
                    total[step, side] += value

    def places(step):
        quarter = step // 2
        x_at = turn(x, quarter + quarter // 2 * (5 - 2 * quarter))
        return x_at, (y_lo + 1 + step % 2) % 2

    def across(step, side):
        return pltpu.make_async_remote_copy(
            src_ref=give.at[step, side], dst_ref=take.at[step, side],
            send_sem=core_send.at[step, side], recv_sem=core_recv.at[step, side],
            device_id=sibling, device_id_type=MESH,
        )

    def out_rows(x_at, y_at):
        return out.at[pl.ds(pl.multiple_of((x_at * AXIS + y_at) * tile, tile), tile)]

    def deliver(step, side, x_at, to_y):
        return pltpu.make_async_remote_copy(
            src_ref=mine.at[step, side], dst_ref=out_rows(x_at, y),
            send_sem=out_send.at[step, side], recv_sem=out_recv.at[y, x_at],
            device_id=device(x, to_y, z, core), device_id_type=MESH,
        )

    def keep(step, side, x_at):
        return pltpu.make_async_copy(mine.at[step, side], out_rows(x_at, y), out_local.at[x_at])

    def finish(step, side):
        x_at, owner_lo = places(step)
        slot = (owner_lo * 2 + core) * (AXIS * AXIS) + x_at * AXIS + y
        factor = -active[slot].astype(jnp.float32)
        across(step, side).wait_recv()
        mine[step, side] = (mine[step, side] + take[step, side]) * factor
        to_y = (y_hi + side) % 2 * 2 + owner_lo

        @pl.when(to_y == y)
        def _():
            keep(step, side, x_at).start()

        @pl.when(to_y != y)
        def _():
            deliver(step, side, x_at, to_y).start()

    last = []

    def units(first, count, side):
        before = last[-1] if last else None

        def body(i):
            step = first + i
            x_at, owner_lo = places(step)
            multiply(x_at, owner_lo * 2 + 1 - core, give, step, side)
            across(step, side).start()
            multiply(x_at, owner_lo * 2 + core, mine, step, side)
            if before is None:

                @pl.when(i > 0)
                def _():
                    finish(step - 1, side)

            else:
                finish(jnp.where(i > 0, step - 1, before[0]), jnp.where(i > 0, side, before[1]))

        pl.loop(0, count)(body)
        last.append((first + count - 1, side))

    split_inverse(y, 0)
    split_inverse(y, 1)
    for way in near:
        way.pass_on()
    for way in near:
        way.turn_off(-1)
    swap.wait_recv()
    for way in pair:
        way.start()
    for way in near:
        way.turned_on(0)
    for way in pair:
        way.turn_off(0)
    for way in near:
        way.turn_off(1)
    for way in near:
        way.passed()
        way.turn_off(2)
    for way in pair:
        way.pass_on()
    for way in pair:
        way.turned_on(0)
    for way in near:
        way.turned_on(-1)
    for way in pair:
        way.turn_off(1)
        way.turn_off(-1)
    for way in pair:
        way.passed()
        way.turn_off(2)
    up_0.wait_recv()
    far_0 = push("inv", inverse_half(turn(y, -1), 0), inverse_half(turn(y, -1), 0), along("y", 1))
    down_1.wait_recv()
    far_1 = push("inv", inverse_half(turn(y, 1), 1), inverse_half(turn(y, 1), 1), along("y", -1))
    split_inverse(turn(y, -1), 0)
    split_inverse(turn(y, 1), 1)
    for by in (1, 2):
        for way in near:
            way.turned_on(by)
    for by in (1, -1):
        for way in pair:
            way.turned_on(by)
    up_1.wait_recv()
    split_inverse(turn(y, -1), 1)
    down_0.wait_recv()
    split_inverse(turn(y, 1), 0)
    for way in both:
        way.arrived(0)
    units(0, 2, 0)
    for way in pair:
        way.turned_on(2)
    for way in near:
        for by in (1, -1, 2):
            way.arrived(by)
    for way in pair:
        way.arrived(1)
    units(2, 2, 0)
    far_0.wait_recv()
    split_inverse(turn(y, 2), 0)
    far_1.wait_recv()
    split_inverse(turn(y, 2), 1)
    units(0, 4, 1)
    for way in pair:
        way.arrived(-1)
    units(4, 2, 0)
    units(4, 2, 1)
    for way in pair:
        way.arrived(2)
    units(6, 2, 0)
    units(6, 2, 1)
    finish(*last[-1])

    steps = give.shape[0]

    def settle(number):
        step, side = number // 2, number % 2
        x_at, owner_lo = places(step)
        to_y = (y_hi + side) % 2 * 2 + owner_lo
        across(step, side).wait_send()

        @pl.when(to_y == y)
        def _():
            keep(step, side, x_at).wait()

        @pl.when(to_y != y)
        def _():
            deliver(step, side, x_at, to_y).wait_send()

    pl.loop(0, steps * 2)(settle)
    for _, copy in sent:
        copy.wait_send()
    for by in range(1, AXIS):
        for x_at in range(AXIS):
            y_at = turn(y, by)
            pltpu.make_async_remote_copy(
                src_ref=mine.at[0, 0], dst_ref=out_rows(x_at, y_at),
                send_sem=out_send.at[0, 0], recv_sem=out_recv.at[y_at, x_at],
                device_id=along("y", by), device_id_type=MESH,
            ).wait_recv()


def on_device(inverse_block, panels, pattern, active):
    rows, tile = inverse_block.shape
    rows_local = rows // tile
    per_group = panels.shape[1] // tile
    steps = AXIS * AXIS // 2
    dma = pltpu.SemaphoreType.DMA
    return pl.pallas_call(
        kernel,
        out_shape=jax.ShapeDtypeStruct((AXIS * AXIS * tile, tile), jnp.float32),
        in_specs=[pl.BlockSpec(memory_space=pl.ANY)] * 2 + [pl.BlockSpec(memory_space=pltpu.SMEM)] * 2,
        out_specs=pl.BlockSpec(memory_space=pl.ANY),
        scratch_shapes=[
            pltpu.VMEM((AXIS, rows_local, tile, tile), jnp.float32),
            pltpu.VMEM((AXIS, rows_local, tile, tile), jnp.bfloat16),
            pltpu.VMEM((AXIS, rows_local, tile, tile), jnp.bfloat16),
            pltpu.VMEM((AXIS, AXIS, 2, per_group, tile, tile), jnp.float32),
            pltpu.VMEM((steps, 2, tile, tile), jnp.float32),
            pltpu.VMEM((steps, 2, tile, tile), jnp.float32),
            pltpu.VMEM((steps, 2, tile, tile), jnp.float32),
            dma((2,)),
            dma((6,)), dma((6,)),
            dma((81,)), dma((81,)),
            dma((steps, 2)), dma((steps, 2)),
            dma((steps, 2)), dma((AXIS, AXIS)), dma((AXIS,)),
        ],
        compiler_params=pltpu.CompilerParams(
            collective_id=0, has_side_effects=True, vmem_limit_bytes=56 * 1024 * 1024
        ),
        cost_estimate=pl.CostEstimate(flops=6 * 128 * tile**3, bytes_accessed=20 * 1024 * 1024, transcendentals=0),
        name="selected_inverse",
    )(
        inverse_block.reshape(rows_local, tile, tile),
        panels.reshape(panels.shape[0], per_group, tile, tile),
        pattern.T,
        active,
    )


def solution(mesh):
    in_specs = (P("row", "col"), P("col", "row", None), P(), P())
    out_specs = P("row", "col")
    return jax.shard_map(
        on_device, mesh=mesh, in_specs=in_specs, out_specs=out_specs, check_vma=False
    )
```

```python
import functools

import jax
import jax.numpy as jnp
from jax import lax
from jax.experimental import pallas as pl
from jax.experimental.pallas import tpu as pltpu
from jax.sharding import PartitionSpec as P

MESH = pl.DeviceIdType.MESH
AXIS = 4


def split(value):
    high = value.astype(jnp.bfloat16)
    low = (value - high.astype(jnp.float32)).astype(jnp.bfloat16)
    return high, low


def kernel(
    inverse_in, panels_in, pattern, active, out,
    inverse, inv_high, inv_low, pan, give, take, mine,
    own_sem, inv_send, inv_recv, pan_send, pan_recv, core_send, core_recv, out_send, out_recv, out_local,
):
    tile = panels_in.shape[3]
    rows_local = inverse_in.shape[0]

    col, row = lax.axis_index("col"), lax.axis_index("row")
    z, x, y_hi = col // (2 * AXIS), col // 2 % AXIS, col % 2
    y_lo, core = row // 2, row % 2
    y = y_hi * 2 + y_lo

    def device(x_at, y_at, z_at, core_at):
        return (z_at * 2 * AXIS + x_at * 2 + y_at // 2, y_at % 2 * 2 + core_at)

    def turn(at, by):
        return (at + by + AXIS) % AXIS

    def along(axis, by):
        if axis == "x":
            return device(turn(x, by), y, z, core)
        if axis == "y":
            return device(x, turn(y, by), z, core)
        return device(x, y, turn(z, by), core)

    y_pair, y_outer, y_far = y_hi * 2 + 1 - y_lo, (1 - y_hi) * 2 + 1 - y_lo, (1 - y_hi) * 2 + y_lo
    to_pair, to_outer, to_far = (device(x, y_at, z, core) for y_at in (y_pair, y_outer, y_far))
    sibling = device(x, y, z, 1 - core)

    barrier = pltpu.get_barrier_semaphore()
    peers = [along("x", 1), along("x", -1), along("z", 1), along("z", -1)]
    peers += [to_pair, to_outer, to_far, sibling]
    for peer in peers:
        pl.semaphore_signal(barrier, inc=1, device_id=peer, device_id_type=MESH)
    pl.semaphore_wait(barrier, len(peers))

    sent = []

    def push(kind, source, target, to):
        sends, receives = (inv_send, inv_recv) if kind == "inv" else (pan_send, pan_recv)
        number = len([entry for entry in sent if entry[0] == kind])
        copy = pltpu.make_async_remote_copy(
            src_ref=source, dst_ref=target, send_sem=sends.at[number], recv_sem=receives.at[number],
            device_id=to, device_id_type=MESH,
        )
        copy.start()
        sent.append((kind, copy))
        return copy

    class Way:
        def __init__(self, group, entry, first, second):
            self.group, self.entry, self.first, self.second = group, entry, first, second
            self.flying = {}

        def view(self, by_first, by_second, half=None):
            by_x, by_z = (by_first, by_second) if self.first == "x" else (by_second, by_first)
            tile_at = pan.at[turn(x, by_x), turn(z, by_z), self.group, self.entry]
            return tile_at if half is None else tile_at.at[pl.ds(half * (tile // 2), tile // 2)]

        def spread(self, key, axis, at, source=None):
            source = self.view(*at) if source is None else source
            self.flying[key] = [push("pan", source, self.view(*at), along(axis, by)) for by in (1, -1)]

        def relay(self, key, axis, at_below, at_above):
            up, down = self.flying[key]
            up.wait_recv()
            below = self.view(*at_below, half=0)
            far_up = push("pan", below, below, along(axis, 1))
            down.wait_recv()
            above = self.view(*at_above, half=1)
            far_down = push("pan", above, above, along(axis, -1))
            self.flying[key] = [far_up, far_down]

        def settle(self, key):
            for copy in self.flying.pop(key):
                copy.wait_recv()

        def start(self, source=None):
            self.spread("first", self.first, (0, 0), source)

        def pass_on(self):
            self.relay("first", self.first, (-1, 0), (1, 0))

        def passed(self):
            self.settle("first")

        def turn_off(self, by, source=None):
            self.spread(by, self.second, (by, 0), source)

        def turned_on(self, by):
            self.relay(by, self.second, (by, -1), (by, 1))

        def arrived(self, by):
            self.settle(by)

    other = 1 - y_lo
    near = [Way(y_lo, 0, "x", "z"), Way(y_lo, 1, "z", "x")]
    pair = [Way(other, 0, "x", "z"), Way(other, 1, "z", "x")]
    both = near + pair

    swap = push("pan", panels_in.at[other], pan.at[x, z, y_lo], to_pair)

    lanes = tile // 2
    cut = rows_local * 5 // 8
    spans = (pl.ds(0, cut), pl.ds(cut, rows_local - cut))

    def columns(part):
        return slice(None) if part is None else slice(part * lanes, (part + 1) * lanes)

    def own(part, span):
        return inverse_in.at[spans[span], :, pl.ds(part * lanes, lanes)]

    def held(part, y_at, span):
        return inverse.at[part, y_at, spans[span]]

    def give_own(part, span, to):
        return push("inv", own(part, span), held(part, y, span), to)

    def relay_inverse(part, span, y_at, to):
        return push("inv", held(part, y_at, span), held(part, y_at, span), to)

    pair_0, outer_0, pair_1, outer_1, far_0, far_1 = ([None, None] for _ in range(6))
    pair_0[0] = give_own(0, 0, to_pair)
    outer_0[0] = give_own(0, 1, to_outer)
    pair_1[0] = give_own(0, 1, to_pair)
    outer_1[0] = give_own(0, 0, to_outer)

    for entry, way in enumerate(near):
        way.start(panels_in.at[y_lo, entry])
    for entry, way in enumerate(near):
        way.turn_off(0, panels_in.at[y_lo, entry])

    own_copies = [
        pltpu.make_async_copy(inverse_in.at[:, :, pl.ds(part * lanes, lanes)], inverse.at[part, y], own_sem.at[part])
        for part in range(2)
    ]
    own_copies.append(pltpu.make_async_copy(panels_in.at[y_lo], pan.at[x, z, y_lo], own_sem.at[2]))
    for copy in own_copies:
        copy.start()
    for copy in own_copies:
        copy.wait()

    def split_inverse(part, y_at, first=0, last=rows_local):
        def body(block):
            high, low = split(inverse[part, y_at, block])
            inv_high[y_at, block, :, columns(part)] = high
            inv_low[y_at, block, :, columns(part)] = low

        pl.loop(first, last)(body)

    def multiply(x_at, z_at, total, step, side, part):
        slot = z_at * (AXIS * AXIS) + x_at * AXIS + y
        column = (y_hi + side) % 2
        at = (step, side, slice(None), columns(part))
        for group in range(2):
            for entry in range(2):
                block = lax.rem(pattern[(group * 2 + core) * 2 + entry, slot], rows_local)
                high, low = split(pan[x_at, z_at, group, entry].T)
                from_high = inv_high[column * 2 + group, block, :, columns(part)]
                from_low = inv_low[column * 2 + group, block, :, columns(part)]
                value = jnp.dot(high, from_high, preferred_element_type=jnp.float32)
                value += jnp.dot(low, from_high, preferred_element_type=jnp.float32)
                value += jnp.dot(high, from_low, preferred_element_type=jnp.float32)
                if group == 0 and entry == 0:
                    total[at] = value
                else:
                    total[at] += value

    def places(step):
        quarter = step // 2
        x_at = turn(x, quarter + quarter // 2 * (5 - 2 * quarter))
        return x_at, (y_lo + 1 + step % 2) % 2

    def cell(ref, step, side, part):
        if part is None:
            return ref.at[step, side]
        return ref.at[step, side, :, pl.ds(part * lanes, lanes)]

    def across(step, side, part):
        return pltpu.make_async_remote_copy(
            src_ref=cell(give, step, side, part), dst_ref=cell(take, step, side, part),
            send_sem=core_send.at[step, side, part or 0], recv_sem=core_recv.at[step, side, part or 0],
            device_id=sibling, device_id_type=MESH,
        )

    def out_rows(x_at, y_at, part):
        rows = out.at[pl.ds(pl.multiple_of((x_at * AXIS + y_at) * tile, tile), tile)]
        return rows if part is None else rows.at[:, pl.ds(part * lanes, lanes)]

    def deliver(step, side, part, x_at, to_y):
        return pltpu.make_async_remote_copy(
            src_ref=cell(mine, step, side, part), dst_ref=out_rows(x_at, y, part),
            send_sem=out_send.at[step, side, part or 0], recv_sem=out_recv.at[y, x_at, part or 0],
            device_id=device(x, to_y, z, core), device_id_type=MESH,
        )

    def keep(step, side, part, x_at):
        return pltpu.make_async_copy(
            cell(mine, step, side, part), out_rows(x_at, y, part), out_local.at[x_at, part or 0]
        )

    def finish(step, side, part):
        x_at, owner_lo = places(step)
        slot = (owner_lo * 2 + core) * (AXIS * AXIS) + x_at * AXIS + y
        factor = -active[slot].astype(jnp.float32)
        across(step, side, part).wait_recv()
        at = (step, side, slice(None), columns(part))
        mine[at] = (mine[at] + take[at]) * factor
        to_y = (y_hi + side) % 2 * 2 + owner_lo

        @pl.when(to_y == y)
        def _():
            keep(step, side, part, x_at).start()

        @pl.when(to_y != y)
        def _():
            deliver(step, side, part, x_at, to_y).start()

    done = []

    def units(first, count, side, part=None):
        before = done[-1] if done else None

        def body(i):
            step = first + i
            x_at, owner_lo = places(step)
            multiply(x_at, owner_lo * 2 + 1 - core, give, step, side, part)
            across(step, side, part).start()
            if before is not None:

                @pl.when(i == 0)
                def _():
                    finish(*before)

            @pl.when(i > 0)
            def _():
                finish(step - 1, side, part)

            multiply(x_at, owner_lo * 2 + core, mine, step, side, part)

        pl.loop(0, count)(body)
        done.append((first + count - 1, side, part))

    def relays(ways, *places_along):
        for by in places_along:
            for way in ways:
                way.turned_on(by)

    def turns(ways, *places_along):
        for by in places_along:
            for way in ways:
                way.turn_off(by)

    def arrivals(ways, *places_along):
        for by in places_along:
            for way in ways:
                way.arrived(by)

    split_inverse(0, y)
    split_inverse(1, y)
    for way in near:
        way.pass_on()
    turns(near, -1)
    outer_0[0].wait_recv()
    far_1[0] = relay_inverse(0, 1, y_outer, to_pair)
    outer_0[1] = give_own(1, 1, to_outer)
    swap.wait_recv()
    for way in pair:
        way.start()
    relays(near, 0)
    turns(pair, 0)
    turns(near, 1)
    for way in near:
        way.passed()
    turns(near, 2)
    pair_0[0].wait_recv()
    far_0[0] = relay_inverse(0, 0, y_pair, to_outer)
    pair_0[1] = give_own(1, 0, to_pair)
    pair_1[1] = give_own(1, 1, to_pair)
    outer_1[1] = give_own(1, 0, to_outer)
    split_inverse(0, y_pair, 0, cut)
    split_inverse(0, y_outer, cut, rows_local)
    for way in pair:
        way.pass_on()
    relays(pair, 0)
    relays(near, -1)
    turns(pair, 1, -1)
    pair_1[0].wait_recv()
    outer_1[0].wait_recv()
    split_inverse(0, y_pair, cut, rows_local)
    split_inverse(0, y_outer, 0, cut)
    outer_0[1].wait_recv()
    far_1[1] = relay_inverse(1, 1, y_outer, to_pair)
    for way in pair:
        way.passed()
    turns(pair, 2)
    relays(near, 1)
    far_1[0].wait_recv()
    far_0[0].wait_recv()
    split_inverse(0, y_far)
    pair_0[1].wait_recv()
    far_0[1] = relay_inverse(1, 0, y_pair, to_outer)
    split_inverse(1, y_pair, 0, cut)
    split_inverse(1, y_outer, cut, rows_local)
    relays(near, 2)
    relays(pair, 1)
    arrivals(both, 0)
    units(0, 2, 1, 0)
    units(0, 2, 0, 0)
    relays(pair, -1)
    pair_1[1].wait_recv()
    outer_1[1].wait_recv()
    split_inverse(1, y_pair, cut, rows_local)
    split_inverse(1, y_outer, 0, cut)
    relays(pair, 2)
    far_0[1].wait_recv()
    far_1[1].wait_recv()
    split_inverse(1, y_far)
    units(0, 2, 1, 1)
    units(0, 2, 0, 1)
    arrivals(near, 1, -1, 2)
    arrivals(pair, 1)
    units(2, 2, 1)
    units(2, 2, 0)
    arrivals(pair, -1)
    units(4, 2, 1)
    units(4, 2, 0)
    arrivals(pair, 2)
    units(6, 2, 1)
    units(6, 2, 0)
    finish(*done[-1])

    steps = give.shape[0]

    def settle(number, parts):
        step, side = number // 2, number % 2
        x_at, owner_lo = places(step)
        to_y = (y_hi + side) % 2 * 2 + owner_lo
        for part in parts:
            across(step, side, part).wait_send()

        @pl.when(to_y == y)
        def _():
            for part in parts:
                keep(step, side, part, x_at).wait()

        @pl.when(to_y != y)
        def _():
            for part in parts:
                deliver(step, side, part, x_at, to_y).wait_send()

    pl.loop(0, 4)(functools.partial(settle, parts=(0, 1)))
    pl.loop(4, steps * 2)(functools.partial(settle, parts=(None,)))
    for _, copy in sent:
        copy.wait_send()
    for y_at in (y_pair, y_outer, y_far):
        for by in range(AXIS):
            x_at = turn(x, by)
            for part in (0, 1) if by == 0 else (None,):
                pltpu.make_async_remote_copy(
                    src_ref=cell(mine, 0, 0, part), dst_ref=out_rows(x_at, y_at, part),
                    send_sem=out_send.at[0, 0, 0], recv_sem=out_recv.at[y_at, x_at, part or 0],
                    device_id=to_pair, device_id_type=MESH,
                ).wait_recv()


def on_device(inverse_block, panels, pattern, active):
    rows, tile = inverse_block.shape
    rows_local = rows // tile
    per_group = panels.shape[1] // tile
    steps = AXIS * AXIS // 2
    dma = pltpu.SemaphoreType.DMA
    return pl.pallas_call(
        kernel,
        out_shape=pltpu.VMEM((AXIS * AXIS * tile, tile), jnp.float32),
        in_specs=[pl.BlockSpec(memory_space=pl.ANY)] * 2 + [pl.BlockSpec(memory_space=pltpu.SMEM)] * 2,
        out_specs=pl.BlockSpec(memory_space=pltpu.VMEM),
        scratch_shapes=[
            pltpu.VMEM((2, AXIS, rows_local, tile, tile // 2), jnp.float32),
            pltpu.VMEM((AXIS, rows_local, tile, tile), jnp.bfloat16),
            pltpu.VMEM((AXIS, rows_local, tile, tile), jnp.bfloat16),
            pltpu.VMEM((AXIS, AXIS, 2, per_group, tile, tile), jnp.float32),
            pltpu.VMEM((steps, 2, tile, tile), jnp.float32),
            pltpu.VMEM((steps, 2, tile, tile), jnp.float32),
            pltpu.VMEM((steps, 2, tile, tile), jnp.float32),
            dma((3,)),
            dma((12,)), dma((12,)),
            dma((81,)), dma((81,)),
            dma((steps, 2, 2)), dma((steps, 2, 2)),
            dma((steps, 2, 2)), dma((AXIS, AXIS, 2)), dma((AXIS, 2)),
        ],
        compiler_params=pltpu.CompilerParams(
            collective_id=0, has_side_effects=True, vmem_limit_bytes=56 * 1024 * 1024
        ),
        cost_estimate=pl.CostEstimate(flops=6 * 128 * tile**3, bytes_accessed=20 * 1024 * 1024, transcendentals=0),
        name="selected_inverse",
    )(
        inverse_block.reshape(rows_local, tile, tile),
        panels.reshape(panels.shape[0], per_group, tile, tile),
        pattern.T,
        active,
    )


def solution(mesh):
    in_specs = (P("row", "col"), P("col", "row", None), P(), P())
    out_specs = P("row", "col")
    return jax.shard_map(
        on_device, mesh=mesh, in_specs=in_specs, out_specs=out_specs, check_vma=False
    )
```

```python
import functools

import jax
import jax.numpy as jnp
from jax import lax
from jax.experimental import pallas as pl
from jax.experimental.pallas import tpu as pltpu
from jax.sharding import PartitionSpec as P

MESH = pl.DeviceIdType.MESH
AXIS = 4


def split(value):
    high = value.astype(jnp.bfloat16)
    low = (value - high.astype(jnp.float32)).astype(jnp.bfloat16)
    return high, low


def kernel(
    inverse_in, panels_in, pattern, active, out,
    inverse, inv_high, inv_low, pan, give, take, mine,
    own_sem, inv_send, inv_recv, pan_send, pan_recv, core_send, core_recv, out_send, out_recv, out_local,
):
    tile = panels_in.shape[3]
    rows_local = inverse_in.shape[0]

    col, row = lax.axis_index("col"), lax.axis_index("row")
    z, x, y_hi = col // (2 * AXIS), col // 2 % AXIS, col % 2
    y_lo, core = row // 2, row % 2
    y = y_hi * 2 + y_lo

    def device(x_at, y_at, z_at, core_at):
        return (z_at * 2 * AXIS + x_at * 2 + y_at // 2, y_at % 2 * 2 + core_at)

    def turn(at, by):
        return (at + by + AXIS) % AXIS

    def along(axis, by):
        if axis == "x":
            return device(turn(x, by), y, z, core)
        if axis == "y":
            return device(x, turn(y, by), z, core)
        return device(x, y, turn(z, by), core)

    y_pair, y_outer, y_far = y_hi * 2 + 1 - y_lo, (1 - y_hi) * 2 + 1 - y_lo, (1 - y_hi) * 2 + y_lo
    to_pair, to_outer, to_far = (device(x, y_at, z, core) for y_at in (y_pair, y_outer, y_far))
    sibling = device(x, y, z, 1 - core)

    barrier = pltpu.get_barrier_semaphore()
    peers = [along("x", 1), along("x", -1), along("z", 1), along("z", -1)]
    peers += [to_pair, to_outer, to_far, sibling]
    for peer in peers:
        pl.semaphore_signal(barrier, inc=1, device_id=peer, device_id_type=MESH)
    pl.semaphore_wait(barrier, len(peers))

    sent = []

    def push(kind, source, target, to):
        sends, receives = (inv_send, inv_recv) if kind == "inv" else (pan_send, pan_recv)
        number = len([entry for entry in sent if entry[0] == kind])
        copy = pltpu.make_async_remote_copy(
            src_ref=source, dst_ref=target, send_sem=sends.at[number], recv_sem=receives.at[number],
            device_id=to, device_id_type=MESH,
        )
        copy.start()
        sent.append((kind, copy))
        return copy

    class Way:
        def __init__(self, group, entry, first, second):
            self.group, self.entry, self.first, self.second = group, entry, first, second
            self.flying = {}

        def view(self, by_first, by_second, half=None):
            by_x, by_z = (by_first, by_second) if self.first == "x" else (by_second, by_first)
            tile_at = pan.at[turn(x, by_x), turn(z, by_z), self.group, self.entry]
            return tile_at if half is None else tile_at.at[pl.ds(half * (tile // 2), tile // 2)]

        def spread(self, key, axis, at, source=None):
            source = self.view(*at) if source is None else source
            self.flying[key] = [push("pan", source, self.view(*at), along(axis, by)) for by in (1, -1)]

        def relay(self, key, axis, at_below, at_above):
            up, down = self.flying[key]
            up.wait_recv()
            below = self.view(*at_below, half=0)
            far_up = push("pan", below, below, along(axis, 1))
            down.wait_recv()
            above = self.view(*at_above, half=1)
            far_down = push("pan", above, above, along(axis, -1))
            self.flying[key] = [far_up, far_down]

        def settle(self, key):
            for copy in self.flying.pop(key):
                copy.wait_recv()

        def start(self, source=None):
            self.spread("first", self.first, (0, 0), source)

        def pass_on(self):
            self.relay("first", self.first, (-1, 0), (1, 0))

        def passed(self):
            self.settle("first")

        def turn_off(self, by, source=None):
            self.spread(by, self.second, (by, 0), source)

        def turned_on(self, by):
            self.relay(by, self.second, (by, -1), (by, 1))

        def arrived(self, by):
            self.settle(by)

    other = 1 - y_lo
    near = [Way(y_lo, 0, "x", "z"), Way(y_lo, 1, "z", "x")]
    pair = [Way(other, 0, "x", "z"), Way(other, 1, "z", "x")]
    both = near + pair

    swap = push("pan", panels_in.at[other], pan.at[x, z, y_lo], to_pair)

    lanes = tile // 2
    cut = rows_local * 5 // 8
    spans = (pl.ds(0, cut), pl.ds(cut, rows_local - cut))

    def columns(part):
        return slice(None) if part is None else slice(part * lanes, (part + 1) * lanes)

    def own(part, span):
        return inverse_in.at[spans[span], :, pl.ds(part * lanes, lanes)]

    def held(part, y_at, span):
        return inverse.at[part, y_at, spans[span]]

    def give_own(part, span, to):
        return push("inv", own(part, span), held(part, y, span), to)

    def relay_inverse(part, span, y_at, to):
        return push("inv", held(part, y_at, span), held(part, y_at, span), to)

    pair_0, outer_0, pair_1, outer_1, far_0, far_1 = ([None, None] for _ in range(6))
    pair_0[0] = give_own(0, 0, to_pair)
    outer_0[0] = give_own(0, 1, to_outer)
    pair_1[0] = give_own(0, 1, to_pair)
    outer_1[0] = give_own(0, 0, to_outer)

    for entry, way in enumerate(near):
        way.start(panels_in.at[y_lo, entry])
    for entry, way in enumerate(near):
        way.turn_off(0, panels_in.at[y_lo, entry])

    own_copies = [
        pltpu.make_async_copy(inverse_in.at[:, :, pl.ds(part * lanes, lanes)], inverse.at[part, y], own_sem.at[part])
        for part in range(2)
    ]
    own_copies.append(pltpu.make_async_copy(panels_in.at[y_lo], pan.at[x, z, y_lo], own_sem.at[2]))
    for copy in own_copies:
        copy.start()
    for copy in own_copies:
        copy.wait()

    def split_inverse(part, y_at, first=0, last=rows_local):
        def body(block):
            high, low = split(inverse[part, y_at, block])
            inv_high[y_at, block, :, columns(part)] = high
            inv_low[y_at, block, :, columns(part)] = low

        pl.loop(first, last)(body)

    def multiply(x_at, z_at, total, step, part):
        slot = z_at * (AXIS * AXIS) + x_at * AXIS + y
        for group in range(2):
            for entry in range(2):
                block = lax.rem(pattern[(group * 2 + core) * 2 + entry, slot], rows_local)
                high, low = split(pan[x_at, z_at, group, entry].T)
                for side in range(2):
                    column = (y_hi + side) % 2
                    from_high = inv_high[column * 2 + group, block, :, columns(part)]
                    from_low = inv_low[column * 2 + group, block, :, columns(part)]
                    value = jnp.dot(high, from_high, preferred_element_type=jnp.float32)
                    value += jnp.dot(low, from_high, preferred_element_type=jnp.float32)
                    value += jnp.dot(high, from_low, preferred_element_type=jnp.float32)
                    at = (step, side, slice(None), columns(part))
                    if group == 0 and entry == 0:
                        total[at] = value
                    else:
                        total[at] += value

    def places(step):
        return turn(x, (0, 1, -1, 2)[step // 2]), (y_lo + 1 + step % 2) % 2

    def cell(ref, step, side, part):
        if part is None:
            return ref.at[step, side]
        return ref.at[step, side, :, pl.ds(part * lanes, lanes)]

    def across(step, side, part):
        return pltpu.make_async_remote_copy(
            src_ref=cell(give, step, side, part), dst_ref=cell(take, step, side, part),
            send_sem=core_send.at[step, side, part or 0], recv_sem=core_recv.at[step, side, part or 0],
            device_id=sibling, device_id_type=MESH,
        )

    def out_rows(x_at, y_at, part):
        rows = out.at[pl.ds(pl.multiple_of((x_at * AXIS + y_at) * tile, tile), tile)]
        return rows if part is None else rows.at[:, pl.ds(part * lanes, lanes)]

    def deliver(step, side, part, x_at, to_y):
        return pltpu.make_async_remote_copy(
            src_ref=cell(mine, step, side, part), dst_ref=out_rows(x_at, y, part),
            send_sem=out_send.at[step, side, part or 0], recv_sem=out_recv.at[y, x_at, part or 0],
            device_id=device(x, to_y, z, core), device_id_type=MESH,
        )

    def keep(step, side, part, x_at):
        return pltpu.make_async_copy(
            cell(mine, step, side, part), out_rows(x_at, y, part), out_local.at[x_at, part or 0]
        )

    def stays(step, side):
        return step % 2 == 1 and side == 0

    def sending(step, side, part):
        x_at, owner_lo = places(step)
        if stays(step, side):
            return keep(step, side, part, x_at)
        return deliver(step, side, part, x_at, (y_hi + side) % 2 * 2 + owner_lo)

    def finish(step, part):
        x_at, owner_lo = places(step)
        slot = (owner_lo * 2 + core) * (AXIS * AXIS) + x_at * AXIS + y
        factor = -active[slot].astype(jnp.float32)
        for side in (1, 0):
            across(step, side, part).wait_recv()
            at = (step, side, slice(None), columns(part))
            mine[at] = (mine[at] + take[at]) * factor
            sending(step, side, part).start()

    done = []

    def unit(step, part=None):
        x_at, owner_lo = places(step)
        multiply(x_at, owner_lo * 2 + 1 - core, give, step, part)
        for side in (1, 0):
            across(step, side, part).start()
        if done:
            finish(*done[-1])
        multiply(x_at, owner_lo * 2 + core, mine, step, part)
        done.append((step, part))

    def relays(ways, *places_along):
        for by in places_along:
            for way in ways:
                way.turned_on(by)

    def turns(ways, *places_along):
        for by in places_along:
            for way in ways:
                way.turn_off(by)

    def arrivals(ways, *places_along):
        for by in places_along:
            for way in ways:
                way.arrived(by)

    split_inverse(0, y)
    split_inverse(1, y)
    for way in near:
        way.pass_on()
    turns(near, -1)
    outer_0[0].wait_recv()
    far_1[0] = relay_inverse(0, 1, y_outer, to_pair)
    outer_0[1] = give_own(1, 1, to_outer)
    swap.wait_recv()
    for way in pair:
        way.start()
    relays(near, 0)
    turns(pair, 0)
    turns(near, 1)
    for way in near:
        way.passed()
    turns(near, 2)
    pair_0[0].wait_recv()
    far_0[0] = relay_inverse(0, 0, y_pair, to_outer)
    pair_0[1] = give_own(1, 0, to_pair)
    pair_1[1] = give_own(1, 1, to_pair)
    outer_1[1] = give_own(1, 0, to_outer)
    split_inverse(0, y_pair, 0, cut)
    split_inverse(0, y_outer, cut, rows_local)
    for way in pair:
        way.pass_on()
    relays(pair, 0)
    relays(near, -1)
    turns(pair, 1, -1)
    pair_1[0].wait_recv()
    outer_1[0].wait_recv()
    split_inverse(0, y_pair, cut, rows_local)
    split_inverse(0, y_outer, 0, cut)
    outer_0[1].wait_recv()
    far_1[1] = relay_inverse(1, 1, y_outer, to_pair)
    for way in pair:
        way.passed()
    turns(pair, 2)
    relays(near, 1)
    far_1[0].wait_recv()
    far_0[0].wait_recv()
    split_inverse(0, y_far)
    pair_0[1].wait_recv()
    far_0[1] = relay_inverse(1, 0, y_pair, to_outer)
    split_inverse(1, y_pair, 0, cut)
    split_inverse(1, y_outer, cut, rows_local)
    relays(near, 2)
    relays(pair, 1)
    arrivals(both, 0)
    unit(0, 0)
    unit(1, 0)
    relays(pair, -1)
    pair_1[1].wait_recv()
    outer_1[1].wait_recv()
    split_inverse(1, y_pair, cut, rows_local)
    split_inverse(1, y_outer, 0, cut)
    relays(pair, 2)
    far_0[1].wait_recv()
    far_1[1].wait_recv()
    split_inverse(1, y_far)
    unit(0, 1)
    unit(1, 1)
    arrivals(near, 1, -1, 2)
    arrivals(pair, 1)
    unit(2)
    unit(3)
    arrivals(pair, -1)
    unit(4)
    unit(5)
    arrivals(pair, 2)
    unit(6)
    unit(7)
    finish(*done[-1])

    for step, part in done:
        for side in (1, 0):
            across(step, side, part).wait_send()
            copy = sending(step, side, part)
            if stays(step, side):
                copy.wait()
            else:
                copy.wait_send()
    for _, copy in sent:
        copy.wait_send()
    for y_at in (y_pair, y_outer, y_far):
        for by in range(AXIS):
            x_at = turn(x, by)
            for part in (0, 1) if by == 0 else (None,):
                pltpu.make_async_remote_copy(
                    src_ref=cell(mine, 0, 0, part), dst_ref=out_rows(x_at, y_at, part),
                    send_sem=out_send.at[0, 0, 0], recv_sem=out_recv.at[y_at, x_at, part or 0],
                    device_id=to_pair, device_id_type=MESH,
                ).wait_recv()


def on_device(inverse_block, panels, pattern, active):
    rows, tile = inverse_block.shape
    rows_local = rows // tile
    per_group = panels.shape[1] // tile
    steps = AXIS * AXIS // 2
    dma = pltpu.SemaphoreType.DMA
    return pl.pallas_call(
        kernel,
        out_shape=pltpu.VMEM((AXIS * AXIS * tile, tile), jnp.float32),
        in_specs=[pl.BlockSpec(memory_space=pl.ANY)] * 2 + [pl.BlockSpec(memory_space=pltpu.SMEM)] * 2,
        out_specs=pl.BlockSpec(memory_space=pltpu.VMEM),
        scratch_shapes=[
            pltpu.VMEM((2, AXIS, rows_local, tile, tile // 2), jnp.float32),
            pltpu.VMEM((AXIS, rows_local, tile, tile), jnp.bfloat16),
            pltpu.VMEM((AXIS, rows_local, tile, tile), jnp.bfloat16),
            pltpu.VMEM((AXIS, AXIS, 2, per_group, tile, tile), jnp.float32),
            pltpu.VMEM((steps, 2, tile, tile), jnp.float32),
            pltpu.VMEM((steps, 2, tile, tile), jnp.float32),
            pltpu.VMEM((steps, 2, tile, tile), jnp.float32),
            dma((3,)),
            dma((12,)), dma((12,)),
            dma((81,)), dma((81,)),
            dma((steps, 2, 2)), dma((steps, 2, 2)),
            dma((steps, 2, 2)), dma((AXIS, AXIS, 2)), dma((AXIS, 2)),
        ],
        compiler_params=pltpu.CompilerParams(
            collective_id=0, has_side_effects=True, vmem_limit_bytes=56 * 1024 * 1024
        ),
        cost_estimate=pl.CostEstimate(flops=6 * 128 * tile**3, bytes_accessed=20 * 1024 * 1024, transcendentals=0),
        name="selected_inverse",
    )(
        inverse_block.reshape(rows_local, tile, tile),
        panels.reshape(panels.shape[0], per_group, tile, tile),
        pattern.T,
        active,
    )


def solution(mesh):
    in_specs = (P("row", "col"), P("col", "row", None), P(), P())
    out_specs = P("row", "col")
    return jax.shard_map(
        on_device, mesh=mesh, in_specs=in_specs, out_specs=out_specs, check_vma=False
    )
```

```python
import functools

import jax
import jax.numpy as jnp
from jax import lax
from jax.experimental import pallas as pl
from jax.experimental.pallas import tpu as pltpu
from jax.sharding import PartitionSpec as P

MESH = pl.DeviceIdType.MESH
AXIS = 4


def split(value):
    high = value.astype(jnp.bfloat16)
    low = (value - high.astype(jnp.float32)).astype(jnp.bfloat16)
    return high, low


def kernel(
    inverse_in, panels_in, pattern, active, out,
    inverse, inv_high, inv_low, pan, far_pan, give, take, mine, far_give, far_take, far_mine,
    own_sem, inv_send, inv_recv, pan_send, pan_recv, core_send, core_recv, far_send, far_recv, out_send, out_recv,
):
    tile = panels_in.shape[3]
    rows_local = inverse_in.shape[0]

    col, row = lax.axis_index("col"), lax.axis_index("row")
    z, x, y_hi = col // (2 * AXIS), col // 2 % AXIS, col % 2
    y_lo, core = row // 2, row % 2
    y = y_hi * 2 + y_lo

    def device(x_at, y_at, z_at, core_at):
        return (z_at * 2 * AXIS + x_at * 2 + y_at // 2, y_at % 2 * 2 + core_at)

    def turn(at, by):
        return (at + by + AXIS) % AXIS

    def along(axis, by):
        if axis == "x":
            return device(turn(x, by), y, z, core)
        if axis == "y":
            return device(x, turn(y, by), z, core)
        return device(x, y, turn(z, by), core)

    y_pair, y_outer, y_far = y_hi * 2 + 1 - y_lo, (1 - y_hi) * 2 + 1 - y_lo, (1 - y_hi) * 2 + y_lo
    to_pair, to_outer, to_far = (device(x, y_at, z, core) for y_at in (y_pair, y_outer, y_far))
    sibling = device(x, y, z, 1 - core)

    barrier = pltpu.get_barrier_semaphore()
    peers = [along("x", 1), along("x", -1), along("z", 1), along("z", -1)]
    peers += [to_pair, to_outer, to_far, sibling]
    for peer in peers:
        pl.semaphore_signal(barrier, inc=1, device_id=peer, device_id_type=MESH)
    pl.semaphore_wait(barrier, len(peers))

    sent = []

    def push(kind, source, target, to):
        sends, receives = (inv_send, inv_recv) if kind == "inv" else (pan_send, pan_recv)
        number = len([entry for entry in sent if entry[0] == kind])
        copy = pltpu.make_async_remote_copy(
            src_ref=source, dst_ref=target, send_sem=sends.at[number], recv_sem=receives.at[number],
            device_id=to, device_id_type=MESH,
        )
        copy.start()
        sent.append((kind, copy))
        return copy

    class Way:
        def __init__(self, hold, first, second):
            self.hold, self.first, self.second = hold, first, second
            self.flying = {}

        def view(self, by_first, by_second, half=None):
            by_x, by_z = (by_first, by_second) if self.first == "x" else (by_second, by_first)
            tile_at = self.hold(turn(x, by_x), turn(z, by_z))
            return tile_at if half is None else tile_at.at[pl.ds(half * (tile // 2), tile // 2)]

        def spread(self, key, axis, at, source=None):
            source = self.view(*at) if source is None else source
            self.flying[key] = [push("pan", source, self.view(*at), along(axis, by)) for by in (1, -1)]

        def relay(self, key, axis, at_below, at_above):
            up, down = self.flying[key]
            up.wait_recv()
            below = self.view(*at_below, half=0)
            far_up = push("pan", below, below, along(axis, 1))
            down.wait_recv()
            above = self.view(*at_above, half=1)
            far_down = push("pan", above, above, along(axis, -1))
            self.flying[key] = [far_up, far_down]

        def settle(self, key):
            for copy in self.flying.pop(key):
                copy.wait_recv()

        def start(self, source=None):
            self.spread("first", self.first, (0, 0), source)

        def pass_on(self):
            self.relay("first", self.first, (-1, 0), (1, 0))

        def passed(self):
            self.settle("first")

        def turn_off(self, by, source=None):
            self.spread(by, self.second, (by, 0), source)

        def turned_on(self, by):
            self.relay(by, self.second, (by, -1), (by, 1))

        def arrived(self, by):
            self.settle(by)

    other = 1 - y_lo
    near = [Way(lambda *at: pan.at[*at, y_lo, 0], "x", "z"), Way(lambda *at: pan.at[*at, y_lo, 1], "z", "x")]
    pair = [Way(lambda *at: pan.at[*at, other, 0], "x", "z"), Way(lambda *at: pan.at[*at, other, 1], "z", "x")]
    far = [Way(lambda *at: far_pan.at[*at, 0], "x", "z"), Way(lambda *at: far_pan.at[*at, 1], "z", "x")]

    swap = push("pan", panels_in.at[other], pan.at[x, z, y_lo], to_pair)

    lanes = tile // 2
    cut = rows_local * 5 // 8
    spans = (pl.ds(0, cut), pl.ds(cut, rows_local - cut))

    def columns(part):
        return slice(None) if part is None else slice(part * lanes, (part + 1) * lanes)

    def own(part, span):
        return inverse_in.at[spans[span], :, pl.ds(part * lanes, lanes)]

    def held(part, y_at, span):
        return inverse.at[part, y_at, spans[span]]

    def give_own(part, span, to):
        return push("inv", own(part, span), held(part, y, span), to)

    def relay_inverse(part, span, y_at, to):
        return push("inv", held(part, y_at, span), held(part, y_at, span), to)

    pair_0, outer_0, pair_1, outer_1, far_0, far_1 = ([None, None] for _ in range(6))
    pair_0[0] = give_own(0, 0, to_pair)
    outer_0[0] = give_own(0, 1, to_outer)
    pair_1[0] = give_own(0, 1, to_pair)
    outer_1[0] = give_own(0, 0, to_outer)

    for entry, way in enumerate(near):
        way.start(panels_in.at[y_lo, entry])
    for entry, way in enumerate(near):
        way.turn_off(0, panels_in.at[y_lo, entry])

    own_copies = [
        pltpu.make_async_copy(inverse_in.at[:, :, pl.ds(part * lanes, lanes)], inverse.at[part, y], own_sem.at[part])
        for part in range(2)
    ]
    own_copies.append(pltpu.make_async_copy(panels_in.at[y_lo], pan.at[x, z, y_lo], own_sem.at[2]))
    for copy in own_copies:
        copy.start()
    for copy in own_copies:
        copy.wait()

    def split_inverse(part, y_at, first=0, last=rows_local):
        def body(block):
            high, low = split(inverse[part, y_at, block])
            inv_high[y_at, block, :, columns(part)] = high
            inv_low[y_at, block, :, columns(part)] = low

        pl.loop(first, last)(body)

    def product(piece, group, entry, slot, outputs):
        block = lax.rem(pattern[(group * 2 + core) * 2 + entry, slot], rows_local)
        high, low = split(piece.T)
        for column, rows, part, total, at in outputs:
            at_inverse = (column * 2 + group, block, slice(None), columns(part))
            from_high, from_low = inv_high[at_inverse], inv_low[at_inverse]
            value = jnp.dot(high[:rows], from_high, preferred_element_type=jnp.float32)
            value += jnp.dot(low[:rows], from_high, preferred_element_type=jnp.float32)
            value += jnp.dot(high[:rows], from_low, preferred_element_type=jnp.float32)
            if group == 0 and entry == 0:
                total[at] = value
            else:
                total[at] += value

    def multiply(x_at, z_at, total, step, part):
        slot = z_at * (AXIS * AXIS) + x_at * AXIS + y
        for group in range(2):
            for entry in range(2):
                outputs = [
                    ((y_hi + side) % 2, height(step, side), part, total, place(step, side, part)) for side in range(2)
                ]
                product(pan[x_at, z_at, group, entry], group, entry, slot, outputs)

    def places(step):
        return turn(x, (0, 1, -1, 2)[step // 2]), (y_lo + 1 + step % 2) % 2

    def stays(step, side):
        return step % 2 == 1 and side == 0

    def height(step, side):
        return tile // 2 if step % 2 == 1 and side == 1 else tile

    def place(step, side, part):
        return step, side, slice(0, height(step, side)), columns(part)

    def cell(ref, step, side, part):
        first, width = (0, tile) if part is None else (part * lanes, lanes)
        return ref.at[step, side, pl.ds(0, height(step, side)), pl.ds(first, width)]

    def across(step, side, part):
        return pltpu.make_async_remote_copy(
            src_ref=cell(give, step, side, part), dst_ref=cell(take, step, side, part),
            send_sem=core_send.at[step, side, part or 0], recv_sem=core_recv.at[step, side, part or 0],
            device_id=sibling, device_id_type=MESH,
        )

    def first_row(x_at, y_at):
        return pl.multiple_of((x_at * AXIS + y_at) * tile, tile)

    def out_cell(x_at, y_at, rows, part):
        first, width = (0, tile) if part is None else (part * lanes, lanes)
        return out.at[pl.ds(first_row(x_at, y_at), rows), pl.ds(first, width)]

    def deliver(step, side, part):
        x_at, owner_lo = places(step)
        return pltpu.make_async_remote_copy(
            src_ref=cell(mine, step, side, part), dst_ref=out_cell(x_at, y, height(step, side), part),
            send_sem=out_send.at[step, side, part or 0], recv_sem=out_recv.at[y, x_at, part or 0],
            device_id=device(x, (y_hi + side) % 2 * 2 + owner_lo, z, core), device_id_type=MESH,
        )

    def factor_of(slot):
        return -active[slot].astype(jnp.float32)

    def finish(step, part):
        x_at, owner_lo = places(step)
        factor = factor_of((owner_lo * 2 + core) * (AXIS * AXIS) + x_at * AXIS + y)
        for side in (1, 0):
            across(step, side, part).wait_recv()
            at = place(step, side, part)
            value = (mine[at] + take[at]) * factor
            if stays(step, side):
                out[pl.ds(first_row(x_at, y), tile), columns(part)] = value
            else:
                mine[at] = value
                deliver(step, side, part).start()

    done = []

    def unit(step, part=None):
        x_at, owner_lo = places(step)
        multiply(x_at, owner_lo * 2 + 1 - core, give, step, part)
        for side in (1, 0):
            across(step, side, part).start()
        if done:
            finish(*done[-1])
        multiply(x_at, owner_lo * 2 + core, mine, step, part)
        done.append((step, part))

    def far_multiply(x_at, z_at, total, number):
        slot = z_at * (AXIS * AXIS) + x_at * AXIS + y_far
        for group in range(2):
            for entry in range(2):
                piece = far_pan[x_at, (1 - group) * 2 + z_at % 2, entry]
                product(piece, group, entry, slot, [(y_hi, tile // 2, None, total, number)])

    def far_across(number):
        return pltpu.make_async_remote_copy(
            src_ref=far_give.at[number], dst_ref=far_take.at[number],
            send_sem=far_send.at[number], recv_sem=far_recv.at[number],
            device_id=sibling, device_id_type=MESH,
        )

    def far_unit(number):
        x_at, _ = places(2 * number)
        far_multiply(x_at, y_lo * 2 + 1 - core, far_give, number)
        far_across(number).start()
        far_multiply(x_at, y_lo * 2 + core, far_mine, number)

    def far_finish(number):
        x_at, _ = places(2 * number)
        factor = factor_of((y_lo * 2 + core) * (AXIS * AXIS) + x_at * AXIS + y_far)
        far_across(number).wait_recv()
        rows = pl.ds(first_row(x_at, y_far) + tile // 2, tile // 2)
        out[rows, :] = (far_mine[number] + far_take[number]) * factor

    def relays(ways, *places_along):
        for by in places_along:
            for way in ways:
                way.turned_on(by)

    def turns(ways, *places_along):
        for by in places_along:
            for way in ways:
                way.turn_off(by)

    def arrivals(ways, *places_along):
        for by in places_along:
            for way in ways:
                way.arrived(by)

    def pass_on(ways):
        for way in ways:
            way.pass_on()

    def passed(ways):
        for way in ways:
            way.passed()

    split_inverse(0, y)
    split_inverse(1, y)
    pass_on(near)
    outer_0[0].wait_recv()
    far_1[0] = relay_inverse(0, 1, y_outer, to_pair)
    outer_0[1] = give_own(1, 1, to_outer)
    swap.wait_recv()
    for way in pair:
        way.start()
    relays(near, 0)
    turns(pair, 0)
    turns(near, -1, 1)
    passed(near)
    turns(near, 2)
    pair_0[0].wait_recv()
    far_0[0] = relay_inverse(0, 0, y_pair, to_outer)
    arrivals(near[:1], 0)
    crossing = push(
        "pan", pan.at[x, y_lo * 2 + z % 2, 1 - z // 2, :, :, pl.ds(tile // 2, tile // 2)], far_pan.at[x, z], to_far
    )
    pair_0[1] = give_own(1, 0, to_pair)
    pair_1[1] = give_own(1, 1, to_pair)
    outer_1[1] = give_own(1, 0, to_outer)
    split_inverse(0, y_pair, 0, cut)
    split_inverse(0, y_outer, cut, rows_local)
    pass_on(pair)
    relays(pair, 0)
    relays(near, -1)
    turns(pair, 1, -1)
    pair_1[0].wait_recv()
    outer_1[0].wait_recv()
    split_inverse(0, y_pair, cut, rows_local)
    split_inverse(0, y_outer, 0, cut)
    outer_0[1].wait_recv()
    far_1[1] = relay_inverse(1, 1, y_outer, to_pair)
    passed(pair)
    turns(pair, 2)
    relays(near, 1)
    far_1[0].wait_recv()
    far_0[0].wait_recv()
    split_inverse(0, y_far)
    crossing.wait_recv()
    for way in far:
        way.start()
    turns(far, 0)
    arrivals(near[1:] + pair, 0)
    pair_0[1].wait_recv()
    far_0[1] = relay_inverse(1, 0, y_pair, to_outer)
    split_inverse(1, y_pair, 0, cut)
    split_inverse(1, y_outer, cut, rows_local)
    relays(near, 2)
    relays(pair, 1)
    unit(0, 0)
    unit(1, 0)
    relays(pair, -1)
    pair_1[1].wait_recv()
    outer_1[1].wait_recv()
    split_inverse(1, y_pair, cut, rows_local)
    split_inverse(1, y_outer, 0, cut)
    relays(pair, 2)
    pass_on(far)
    turns(far, -1, 1)
    relays(far, 0)
    far_0[1].wait_recv()
    far_1[1].wait_recv()
    split_inverse(1, y_far)
    unit(0, 1)
    unit(1, 1)
    arrivals(near, 1, -1, 2)
    arrivals(pair, 1)
    unit(2)
    unit(3)
    arrivals(pair, -1)
    unit(4)
    unit(5)
    passed(far)
    turns(far, 2)
    relays(far, -1, 1)
    arrivals(pair, 2)
    unit(6)
    relays(far, 2)
    unit(7)
    finish(*done[-1])
    arrivals(far, 0)
    far_unit(0)
    for number, by in enumerate((1, -1, 2), 1):
        arrivals(far, by)
        far_unit(number)
        far_finish(number - 1)
    far_finish(number)
    for number in range(AXIS):
        far_across(number).wait_send()
    for step, part in done:
        for side in (1, 0):
            across(step, side, part).wait_send()
            if not stays(step, side):
                deliver(step, side, part).wait_send()
    for _, copy in sent:
        copy.wait_send()
    for y_at in (y_pair, y_outer, y_far):
        rows = tile // 2 if y_at is y_far else tile
        for by in range(AXIS):
            x_at = turn(x, by)
            for part in (0, 1) if by == 0 else (None,):
                first, width = (0, tile) if part is None else (part * lanes, lanes)
                pltpu.make_async_remote_copy(
                    src_ref=mine.at[0, 0, pl.ds(0, rows), pl.ds(first, width)],
                    dst_ref=out_cell(x_at, y_at, rows, part),
                    send_sem=out_send.at[0, 0, 0], recv_sem=out_recv.at[y_at, x_at, part or 0],
                    device_id=to_pair, device_id_type=MESH,
                ).wait_recv()


def on_device(inverse_block, panels, pattern, active):
    rows, tile = inverse_block.shape
    rows_local = rows // tile
    per_group = panels.shape[1] // tile
    steps = AXIS * AXIS // 2
    dma = pltpu.SemaphoreType.DMA
    return pl.pallas_call(
        kernel,
        out_shape=pltpu.VMEM((AXIS * AXIS * tile, tile), jnp.float32),
        in_specs=[pl.BlockSpec(memory_space=pl.ANY)] * 2 + [pl.BlockSpec(memory_space=pltpu.SMEM)] * 2,
        out_specs=pl.BlockSpec(memory_space=pltpu.VMEM),
        scratch_shapes=[
            pltpu.VMEM((2, AXIS, rows_local, tile, tile // 2), jnp.float32),
            pltpu.VMEM((AXIS, rows_local, tile, tile), jnp.bfloat16),
            pltpu.VMEM((AXIS, rows_local, tile, tile), jnp.bfloat16),
            pltpu.VMEM((AXIS, AXIS, 2, per_group, tile, tile), jnp.float32),
            pltpu.VMEM((AXIS, AXIS, per_group, tile, tile // 2), jnp.float32),
            pltpu.VMEM((steps, 2, tile, tile), jnp.float32),
            pltpu.VMEM((steps, 2, tile, tile), jnp.float32),
            pltpu.VMEM((steps, 2, tile, tile), jnp.float32),
            pltpu.VMEM((AXIS, tile // 2, tile), jnp.float32),
            pltpu.VMEM((AXIS, tile // 2, tile), jnp.float32),
            pltpu.VMEM((AXIS, tile // 2, tile), jnp.float32),
            dma((3,)),
            dma((12,)), dma((12,)),
            dma((122,)), dma((122,)),
            dma((steps, 2, 2)), dma((steps, 2, 2)),
            dma((AXIS,)), dma((AXIS,)),
            dma((steps, 2, 2)), dma((AXIS, AXIS, 2)),
        ],
        compiler_params=pltpu.CompilerParams(
            collective_id=0, has_side_effects=True, vmem_limit_bytes=56 * 1024 * 1024
        ),
        cost_estimate=pl.CostEstimate(flops=6 * 128 * tile**3, bytes_accessed=20 * 1024 * 1024, transcendentals=0),
        name="selected_inverse",
    )(
        inverse_block.reshape(rows_local, tile, tile),
        panels.reshape(panels.shape[0], per_group, tile, tile),
        pattern.T,
        active,
    )


def solution(mesh):
    in_specs = (P("row", "col"), P("col", "row", None), P(), P())
    out_specs = P("row", "col")
    return jax.shard_map(
        on_device, mesh=mesh, in_specs=in_specs, out_specs=out_specs, check_vma=False
    )
```

```python
import functools

import jax
import jax.numpy as jnp
from jax import lax
from jax.experimental import pallas as pl
from jax.experimental.pallas import tpu as pltpu
from jax.sharding import PartitionSpec as P

MESH = pl.DeviceIdType.MESH
AXIS = 4


def split(value):
    high = value.astype(jnp.bfloat16)
    low = (value - high.astype(jnp.float32)).astype(jnp.bfloat16)
    return high, low


def kernel(
    inverse_in, panels_in, pattern, active, out,
    inverse, inv_high, inv_low, pan, far_pan, give, take, mine, far_give, far_take, far_mine,
    own_sem, inv_send, inv_recv, pan_send, pan_recv, core_send, core_recv, far_send, far_recv, out_send, out_recv,
):
    tile = panels_in.shape[3]
    rows_local = inverse_in.shape[0]

    col, row = lax.axis_index("col"), lax.axis_index("row")
    z, x, y_hi = col // (2 * AXIS), col // 2 % AXIS, col % 2
    y_lo, core = row // 2, row % 2
    y = y_hi * 2 + y_lo

    def device(x_at, y_at, z_at, core_at):
        return (z_at * 2 * AXIS + x_at * 2 + y_at // 2, y_at % 2 * 2 + core_at)

    def turn(at, by):
        return (at + by + AXIS) % AXIS

    def along(axis, by):
        if axis == "x":
            return device(turn(x, by), y, z, core)
        if axis == "y":
            return device(x, turn(y, by), z, core)
        return device(x, y, turn(z, by), core)

    y_pair, y_outer, y_far = y_hi * 2 + 1 - y_lo, (1 - y_hi) * 2 + 1 - y_lo, (1 - y_hi) * 2 + y_lo
    to_pair, to_outer, to_far = (device(x, y_at, z, core) for y_at in (y_pair, y_outer, y_far))
    sibling = device(x, y, z, 1 - core)

    barrier = pltpu.get_barrier_semaphore()
    peers = [along("x", 1), along("x", -1), along("z", 1), along("z", -1)]
    peers += [to_pair, to_outer, to_far, sibling]
    for peer in peers:
        pl.semaphore_signal(barrier, inc=1, device_id=peer, device_id_type=MESH)
    pl.semaphore_wait(barrier, len(peers))

    sent = []

    def push(kind, source, target, to):
        sends, receives = (inv_send, inv_recv) if kind == "inv" else (pan_send, pan_recv)
        number = len([entry for entry in sent if entry[0] == kind])
        copy = pltpu.make_async_remote_copy(
            src_ref=source, dst_ref=target, send_sem=sends.at[number], recv_sem=receives.at[number],
            device_id=to, device_id_type=MESH,
        )
        copy.start()
        sent.append((kind, copy))
        return copy

    received = []

    def got(*copies):
        for copy in copies:
            if not any(copy is known for known in received):
                copy.wait_recv()
                received.append(copy)

    class Way:
        def __init__(self, hold, first, second):
            self.hold, self.first, self.second = hold, first, second
            self.next_to, self.beyond = {}, {}

        def view(self, by_first, by_second, half=None):
            by_x, by_z = (by_first, by_second) if self.first == "x" else (by_second, by_first)
            tile_at = self.hold(turn(x, by_x), turn(z, by_z))
            return tile_at if half is None else tile_at.at[pl.ds(half * (tile // 2), tile // 2)]

        def spread(self, key, axis, at, source=None):
            source = self.view(*at) if source is None else source
            self.next_to[key] = [push("pan", source, self.view(*at), along(axis, by)) for by in (1, -1)]

        def relay(self, key, axis, at_below, at_above):
            up, down = self.next_to[key]
            got(up)
            below = self.view(*at_below, half=0)
            far_up = push("pan", below, below, along(axis, 1))
            got(down)
            above = self.view(*at_above, half=1)
            self.beyond[key] = [far_up, push("pan", above, above, along(axis, -1))]

        def start(self, source=None):
            self.spread("first", self.first, (0, 0), source)

        def on(self):
            self.relay("first", self.first, (-1, 0), (1, 0))

        def turn_off(self, by, source=None):
            if by == 2:
                got(*self.beyond["first"])
            elif by != 0:
                got(*self.next_to["first"])
            self.spread(by, self.second, (by, 0), source)

        def on_again(self, by):
            self.relay(by, self.second, (by, -1), (by, 1))

    other = 1 - y_lo
    near = [Way(lambda *at: pan.at[*at, y_lo, 0], "x", "z"), Way(lambda *at: pan.at[*at, y_lo, 1], "z", "x")]
    pair = [Way(lambda *at: pan.at[*at, other, 0], "x", "z"), Way(lambda *at: pan.at[*at, other, 1], "z", "x")]
    far = [Way(lambda *at: far_pan.at[*at, 0], "x", "z"), Way(lambda *at: far_pan.at[*at, 1], "z", "x")]

    def arrived(ways, by):
        along_x, along_z = ways
        got(*along_x.beyond[by])
        if by == 0:
            got(*along_z.beyond["first"])
        else:
            for at in (0, -1, 1, 2):
                got(*(along_z.beyond if by == 2 else along_z.next_to)[at])

    lanes = tile // 2
    cut = rows_local * 5 // 8
    spans = (pl.ds(0, cut), pl.ds(cut, rows_local - cut))

    def columns(part):
        return slice(None) if part is None else slice(part * lanes, (part + 1) * lanes)

    def own(part, span):
        return inverse_in.at[spans[span], :, pl.ds(part * lanes, lanes)]

    def held(part, y_at, span):
        return inverse.at[part, y_at, spans[span]]

    def give_own(part, span, to):
        return push("inv", own(part, span), held(part, y, span), to)

    def relay_inverse(part, span, y_at, to):
        return push("inv", held(part, y_at, span), held(part, y_at, span), to)

    pair_0, outer_0, pair_1, outer_1, far_0, far_1 = ([None, None] for _ in range(6))
    own_copies = [
        pltpu.make_async_copy(inverse_in.at[:, :, pl.ds(part * lanes, lanes)], inverse.at[part, y], own_sem.at[part])
        for part in range(2)
    ]
    own_copies.append(pltpu.make_async_copy(panels_in.at[y_lo], pan.at[x, z, y_lo], own_sem.at[2]))
    def split_inverse(part, y_at, first=0, last=rows_local):
        def body(block):
            high, low = split(inverse[part, y_at, block])
            inv_high[y_at, block, :, columns(part)] = high
            inv_low[y_at, block, :, columns(part)] = low

        pl.loop(first, last)(body)

    def split_own():
        for copy in own_copies:
            copy.start()
        for copy in own_copies:
            copy.wait()
        split_inverse(0, y)
        split_inverse(1, y)

    def split_next(part):
        got(pair_0[part], outer_0[part])
        split_inverse(part, y_pair, 0, cut)
        split_inverse(part, y_outer, cut, rows_local)

    def split_rest(part):
        got(pair_1[part], outer_1[part])
        split_inverse(part, y_pair, cut, rows_local)
        split_inverse(part, y_outer, 0, cut)

    def split_far(part):
        got(far_0[part], far_1[part])
        split_inverse(part, y_far)

    def to_far_by_pair(part):
        got(pair_0[part])
        far_0[part] = relay_inverse(part, 0, y_pair, to_outer)

    def to_far_by_outer(part):
        got(outer_0[part])
        far_1[part] = relay_inverse(part, 1, y_outer, to_pair)

    def product(piece, group, entry, slot, outputs):
        block = lax.rem(pattern[(group * 2 + core) * 2 + entry, slot], rows_local)
        high, low = split(piece.T)
        for column, rows, part, total, at in outputs:
            at_inverse = (column * 2 + group, block, slice(None), columns(part))
            from_high, from_low = inv_high[at_inverse], inv_low[at_inverse]
            value = jnp.dot(high[:rows], from_high, preferred_element_type=jnp.float32)
            value += jnp.dot(low[:rows], from_high, preferred_element_type=jnp.float32)
            value += jnp.dot(high[:rows], from_low, preferred_element_type=jnp.float32)
            if group == 0 and entry == 0:
                total[at] = value
            else:
                total[at] += value

    def multiply(x_at, z_at, total, step, part):
        slot = z_at * (AXIS * AXIS) + x_at * AXIS + y
        for group in range(2):
            for entry in range(2):
                outputs = [
                    ((y_hi + side) % 2, height(step, side), part, total, place(step, side, part)) for side in range(2)
                ]
                product(pan[x_at, z_at, group, entry], group, entry, slot, outputs)

    def places(step):
        return turn(x, (0, 1, -1, 2)[step // 2]), (y_lo + 1 + step % 2) % 2

    def stays(step, side):
        return step % 2 == 1 and side == 0

    def height(step, side):
        return tile // 2 if step % 2 == 1 and side == 1 else tile

    def place(step, side, part):
        return step, side, slice(0, height(step, side)), columns(part)

    def cell(ref, step, side, part):
        first, width = (0, tile) if part is None else (part * lanes, lanes)
        return ref.at[step, side, pl.ds(0, height(step, side)), pl.ds(first, width)]

    def across(step, side, part):
        return pltpu.make_async_remote_copy(
            src_ref=cell(give, step, side, part), dst_ref=cell(take, step, side, part),
            send_sem=core_send.at[step, side, part or 0], recv_sem=core_recv.at[step, side, part or 0],
            device_id=sibling, device_id_type=MESH,
        )

    def first_row(x_at, y_at):
        return pl.multiple_of((x_at * AXIS + y_at) * tile, tile)

    def out_cell(x_at, y_at, rows, part):
        first, width = (0, tile) if part is None else (part * lanes, lanes)
        return out.at[pl.ds(first_row(x_at, y_at), rows), pl.ds(first, width)]

    def deliver(step, side, part):
        x_at, owner_lo = places(step)
        return pltpu.make_async_remote_copy(
            src_ref=cell(mine, step, side, part), dst_ref=out_cell(x_at, y, height(step, side), part),
            send_sem=out_send.at[step, side, part or 0], recv_sem=out_recv.at[y, x_at, part or 0],
            device_id=device(x, (y_hi + side) % 2 * 2 + owner_lo, z, core), device_id_type=MESH,
        )

    def factor_of(slot):
        return -active[slot].astype(jnp.float32)

    def finish(step, part):
        x_at, owner_lo = places(step)
        factor = factor_of((owner_lo * 2 + core) * (AXIS * AXIS) + x_at * AXIS + y)
        for side in (1, 0):
            across(step, side, part).wait_recv()
            at = place(step, side, part)
            value = (mine[at] + take[at]) * factor
            if stays(step, side):
                out[pl.ds(first_row(x_at, y), tile), columns(part)] = value
            else:
                mine[at] = value
                deliver(step, side, part).start()

    done = []
    pending = []

    def flush():
        while pending:
            pending.pop()()

    def unit(step, part=None):
        x_at, owner_lo = places(step)
        by = (0, 1, -1, 2)[step // 2]
        arrived(near, by)
        arrived(pair, by)
        multiply(x_at, owner_lo * 2 + 1 - core, give, step, part)
        for side in (1, 0):
            across(step, side, part).start()
        flush()
        multiply(x_at, owner_lo * 2 + core, mine, step, part)
        done.append((step, part))
        pending.append(functools.partial(finish, step, part))

    def far_multiply(x_at, z_at, total, number):
        slot = z_at * (AXIS * AXIS) + x_at * AXIS + y_far
        for group in range(2):
            for entry in range(2):
                piece = far_pan[x_at, (1 - group) * 2 + z_at % 2, entry]
                product(piece, group, entry, slot, [(y_hi, tile // 2, None, total, number)])

    def far_across(number):
        return pltpu.make_async_remote_copy(
            src_ref=far_give.at[number], dst_ref=far_take.at[number],
            send_sem=far_send.at[number], recv_sem=far_recv.at[number],
            device_id=sibling, device_id_type=MESH,
        )

    def far_unit(number):
        x_at, _ = places(2 * number)
        arrived(far, (0, 1, -1, 2)[number])
        far_multiply(x_at, y_lo * 2 + 1 - core, far_give, number)
        far_across(number).start()
        flush()
        far_multiply(x_at, y_lo * 2 + core, far_mine, number)
        pending.append(functools.partial(far_finish, number))

    def far_finish(number):
        x_at, _ = places(2 * number)
        factor = factor_of((y_lo * 2 + core) * (AXIS * AXIS) + x_at * AXIS + y_far)
        far_across(number).wait_recv()
        rows = pl.ds(first_row(x_at, y_far) + tile // 2, tile // 2)
        out[rows, :] = (far_mine[number] + far_take[number]) * factor

    outer_0[0] = give_own(0, 1, to_outer)
    swap = push("pan", panels_in.at[other], pan.at[x, z, y_lo], to_pair)
    outer_1[1] = give_own(1, 0, to_outer)
    near[1].start(panels_in.at[y_lo, 1])
    near[0].start(panels_in.at[y_lo, 0])
    split_own()
    near[0].turn_off(0, panels_in.at[y_lo, 0])
    near[1].turn_off(0, panels_in.at[y_lo, 1])
    near[1].turn_off(-1)
    near[1].on()
    near[0].turn_off(-1)
    pair_0[0] = give_own(0, 0, to_pair)
    outer_1[0] = give_own(0, 0, to_outer)
    near[0].on_again(0)
    got(swap)
    pair[1].start()
    pair_1[1] = give_own(1, 1, to_pair)
    got(swap)
    pair[0].start()
    near[1].turn_off(2)
    near[1].on_again(0)
    near[0].turn_off(1)
    pair[0].turn_off(1)
    got(swap, *near[0].beyond[0], *near[1].beyond["first"])
    crossing = push(
        "pan", pan.at[x, y_lo * 2 + z % 2, 1 - z // 2, :, :, pl.ds(tile // 2, tile // 2)], far_pan.at[x, z], to_far
    )
    got(swap)
    pair[1].turn_off(0)
    pair[1].on()
    pair_0[1] = give_own(1, 0, to_pair)
    got(swap)
    pair[0].turn_off(0)
    pair[1].turn_off(-1)
    pair[1].turn_off(1)
    to_far_by_pair(0)
    pair[1].turn_off(2)
    near[0].on_again(-1)
    pair_1[0] = give_own(0, 1, to_pair)
    pair[0].on()
    split_next(0)
    near[1].turn_off(1)
    pair[0].turn_off(-1)
    outer_0[1] = give_own(1, 1, to_outer)
    to_far_by_outer(0)
    got(crossing)
    far[1].start()
    pair[0].on_again(0)
    near[0].on_again(1)
    split_rest(1)
    pair[0].turn_off(2)
    got(crossing)
    far[0].start()
    to_far_by_pair(1)
    near[0].on()
    pair[1].on_again(0)
    got(crossing)
    far[1].turn_off(0)
    to_far_by_outer(1)
    pair[0].on_again(-1)
    pair[0].on_again(1)
    split_next(1)
    split_rest(0)
    pair[1].on_again(2)
    far[1].on()
    split_far(0)
    near[1].on_again(1)
    unit(0, 0)
    unit(1, 0)
    flush()
    near[0].turn_off(2)
    far[0].on()
    pair[1].on_again(-1)
    split_far(1)
    near[1].on_again(2)
    unit(0, 1)
    flush()
    pair[0].on_again(2)
    unit(2)
    flush()
    near[1].on_again(-1)
    far[1].turn_off(-1)
    got(crossing)
    far[0].turn_off(0)
    pair[1].on_again(1)
    far[0].turn_off(-1)
    unit(3)
    unit(1, 1)
    unit(4)
    flush()
    near[0].on_again(2)
    unit(5)
    flush()
    far[0].turn_off(1)
    far[1].turn_off(2)
    far[1].on_again(-1)
    far[0].turn_off(2)
    far[1].turn_off(1)
    far[0].on_again(-1)
    unit(6)
    flush()
    far[0].on_again(1)
    far[0].on_again(0)
    far[1].on_again(2)
    far[1].on_again(0)
    unit(7)
    flush()
    far[1].on_again(1)
    far[0].on_again(2)
    far_unit(2)
    far_unit(1)
    far_unit(0)
    far_unit(3)
    flush()
    for number in range(AXIS):
        far_across(number).wait_send()
    for step, part in done:
        for side in (1, 0):
            across(step, side, part).wait_send()
            if not stays(step, side):
                deliver(step, side, part).wait_send()
    for _, copy in sent:
        got(copy)
        copy.wait_send()
    for y_at in (y_pair, y_outer, y_far):
        rows = tile // 2 if y_at is y_far else tile
        for by in range(AXIS):
            x_at = turn(x, by)
            for part in (0, 1) if by == 0 else (None,):
                first, width = (0, tile) if part is None else (part * lanes, lanes)
                pltpu.make_async_remote_copy(
                    src_ref=mine.at[0, 0, pl.ds(0, rows), pl.ds(first, width)],
                    dst_ref=out_cell(x_at, y_at, rows, part),
                    send_sem=out_send.at[0, 0, 0], recv_sem=out_recv.at[y_at, x_at, part or 0],
                    device_id=to_pair, device_id_type=MESH,
                ).wait_recv()


def on_device(inverse_block, panels, pattern, active):
    rows, tile = inverse_block.shape
    rows_local = rows // tile
    per_group = panels.shape[1] // tile
    steps = AXIS * AXIS // 2
    dma = pltpu.SemaphoreType.DMA
    return pl.pallas_call(
        kernel,
        out_shape=pltpu.VMEM((AXIS * AXIS * tile, tile), jnp.float32),
        in_specs=[pl.BlockSpec(memory_space=pl.ANY)] * 2 + [pl.BlockSpec(memory_space=pltpu.SMEM)] * 2,
        out_specs=pl.BlockSpec(memory_space=pltpu.VMEM),
        scratch_shapes=[
            pltpu.VMEM((2, AXIS, rows_local, tile, tile // 2), jnp.float32),
            pltpu.VMEM((AXIS, rows_local, tile, tile), jnp.bfloat16),
            pltpu.VMEM((AXIS, rows_local, tile, tile), jnp.bfloat16),
            pltpu.VMEM((AXIS, AXIS, 2, per_group, tile, tile), jnp.float32),
            pltpu.VMEM((AXIS, AXIS, per_group, tile, tile // 2), jnp.float32),
            pltpu.VMEM((steps, 2, tile, tile), jnp.float32),
            pltpu.VMEM((steps, 2, tile, tile), jnp.float32),
            pltpu.VMEM((steps, 2, tile, tile), jnp.float32),
            pltpu.VMEM((AXIS, tile // 2, tile), jnp.float32),
            pltpu.VMEM((AXIS, tile // 2, tile), jnp.float32),
            pltpu.VMEM((AXIS, tile // 2, tile), jnp.float32),
            dma((3,)),
            dma((12,)), dma((12,)),
            dma((122,)), dma((122,)),
            dma((steps, 2, 2)), dma((steps, 2, 2)),
            dma((AXIS,)), dma((AXIS,)),
            dma((steps, 2, 2)), dma((AXIS, AXIS, 2)),
        ],
        compiler_params=pltpu.CompilerParams(
            collective_id=0, has_side_effects=True, vmem_limit_bytes=56 * 1024 * 1024
        ),
        cost_estimate=pl.CostEstimate(flops=6 * 128 * tile**3, bytes_accessed=20 * 1024 * 1024, transcendentals=0),
        name="selected_inverse",
    )(
        inverse_block.reshape(rows_local, tile, tile),
        panels.reshape(panels.shape[0], per_group, tile, tile),
        pattern.T,
        active,
    )


def solution(mesh):
    in_specs = (P("row", "col"), P("col", "row", None), P(), P())
    out_specs = P("row", "col")
    return jax.shard_map(
        on_device, mesh=mesh, in_specs=in_specs, out_specs=out_specs, check_vma=False
    )
```

```python
import functools

import jax
import jax.numpy as jnp
from jax import lax
from jax.experimental import pallas as pl
from jax.experimental.pallas import tpu as pltpu
from jax.sharding import PartitionSpec as P

MESH = pl.DeviceIdType.MESH
AXIS = 4


def split(value):
    high = value.astype(jnp.bfloat16)
    low = (value - high.astype(jnp.float32)).astype(jnp.bfloat16)
    return high, low


def kernel(
    inverse_in, panels_in, pattern, active, out,
    inverse, inv_high, inv_low, pan, far_pan, give, take, mine, far_give, far_take, far_mine,
    own_sem, inv_send, inv_recv, pan_send, pan_recv, core_send, core_recv, far_send, far_recv, out_send, out_recv,
):
    tile = panels_in.shape[3]
    rows_local = inverse_in.shape[0]

    col, row = lax.axis_index("col"), lax.axis_index("row")
    z, x, y_hi = col // (2 * AXIS), col // 2 % AXIS, col % 2
    y_lo, core = row // 2, row % 2
    y = y_hi * 2 + y_lo

    def device(x_at, y_at, z_at, core_at):
        return (z_at * 2 * AXIS + x_at * 2 + y_at // 2, y_at % 2 * 2 + core_at)

    def turn(at, by):
        return (at + by + AXIS) % AXIS

    def along(axis, by):
        if axis == "x":
            return device(turn(x, by), y, z, core)
        if axis == "y":
            return device(x, turn(y, by), z, core)
        return device(x, y, turn(z, by), core)

    y_pair, y_outer, y_far = y_hi * 2 + 1 - y_lo, (1 - y_hi) * 2 + 1 - y_lo, (1 - y_hi) * 2 + y_lo
    to_pair, to_outer, to_far = (device(x, y_at, z, core) for y_at in (y_pair, y_outer, y_far))
    sibling = device(x, y, z, 1 - core)

    barrier = pltpu.get_barrier_semaphore()
    peers = [along("x", 1), along("x", -1), along("z", 1), along("z", -1)]
    peers += [to_pair, to_outer, to_far, sibling]
    for peer in peers:
        pl.semaphore_signal(barrier, inc=1, device_id=peer, device_id_type=MESH)
    pl.semaphore_wait(barrier, len(peers))

    sent = []

    def push(kind, source, target, to):
        sends, receives = (inv_send, inv_recv) if kind == "inv" else (pan_send, pan_recv)
        number = len([entry for entry in sent if entry[0] == kind])
        copy = pltpu.make_async_remote_copy(
            src_ref=source, dst_ref=target, send_sem=sends.at[number], recv_sem=receives.at[number],
            device_id=to, device_id_type=MESH,
        )
        copy.start()
        sent.append((kind, copy))
        return copy

    received = []

    def got(*copies):
        for copy in copies:
            if not any(copy is known for known in received):
                copy.wait_recv()
                received.append(copy)

    class Way:
        def __init__(self, hold, first, second):
            self.hold, self.first, self.second = hold, first, second
            self.next_to, self.beyond = {}, {}

        def view(self, by_first, by_second, half=None):
            by_x, by_z = (by_first, by_second) if self.first == "x" else (by_second, by_first)
            tile_at = self.hold(turn(x, by_x), turn(z, by_z))
            return tile_at if half is None else tile_at.at[pl.ds(half * (tile // 2), tile // 2)]

        def spread(self, key, axis, at, source=None):
            source = self.view(*at) if source is None else source
            self.next_to[key] = [push("pan", source, self.view(*at), along(axis, by)) for by in (1, -1)]

        def relay(self, key, axis, at_below, at_above):
            up, down = self.next_to[key]
            got(up)
            below = self.view(*at_below, half=0)
            far_up = push("pan", below, below, along(axis, 1))
            got(down)
            above = self.view(*at_above, half=1)
            self.beyond[key] = [far_up, push("pan", above, above, along(axis, -1))]

        def start(self, source=None):
            self.spread("first", self.first, (0, 0), source)

        def on(self):
            self.relay("first", self.first, (-1, 0), (1, 0))

        def turn_off(self, by, source=None):
            if by == 2:
                got(*self.beyond["first"])
            elif by != 0:
                got(*self.next_to["first"])
            self.spread(by, self.second, (by, 0), source)

        def on_again(self, by):
            self.relay(by, self.second, (by, -1), (by, 1))

    other = 1 - y_lo
    near = [Way(lambda *at: pan.at[*at, y_lo, 0], "x", "z"), Way(lambda *at: pan.at[*at, y_lo, 1], "z", "x")]
    pair = [Way(lambda *at: pan.at[*at, other, 0], "x", "z"), Way(lambda *at: pan.at[*at, other, 1], "z", "x")]
    far = [Way(lambda *at: far_pan.at[*at, 0], "x", "z"), Way(lambda *at: far_pan.at[*at, 1], "z", "x")]

    def arrived(ways, by):
        along_x, along_z = ways
        got(*along_x.beyond[by])
        if by == 0:
            got(*along_z.beyond["first"])
        else:
            for at in (0, -1, 1, 2):
                got(*(along_z.beyond if by == 2 else along_z.next_to)[at])

    lanes = tile // 2
    cuts = (rows_local * 4 // 8, rows_local * 6 // 8)

    def span_of(part, span):
        return (pl.ds(0, cuts[part]), pl.ds(cuts[part], rows_local - cuts[part]))[span]

    def columns(part):
        return slice(None) if part is None else slice(part * lanes, (part + 1) * lanes)

    def own(part, span):
        return inverse_in.at[span_of(part, span), :, pl.ds(part * lanes, lanes)]

    def held(part, y_at, span):
        return inverse.at[part, y_at, span_of(part, span)]

    def give_own(part, span, to):
        return push("inv", own(part, span), held(part, y, span), to)

    def relay_inverse(part, span, y_at, to):
        return push("inv", held(part, y_at, span), held(part, y_at, span), to)

    pair_0, outer_0, pair_1, outer_1, far_0, far_1 = ([None, None] for _ in range(6))
    own_copies = [
        pltpu.make_async_copy(inverse_in.at[:, :, pl.ds(part * lanes, lanes)], inverse.at[part, y], own_sem.at[part])
        for part in range(2)
    ]
    own_copies.append(pltpu.make_async_copy(panels_in.at[y_lo], pan.at[x, z, y_lo], own_sem.at[2]))
    def split_inverse(part, y_at, first=0, last=rows_local):
        def body(block):
            high, low = split(inverse[part, y_at, block])
            inv_high[y_at, block, :, columns(part)] = high
            inv_low[y_at, block, :, columns(part)] = low

        pl.loop(first, last)(body)

    def split_own():
        for copy in own_copies:
            copy.start()
        for copy in own_copies:
            copy.wait()
        split_inverse(0, y)
        split_inverse(1, y)

    def split_next(part):
        got(pair_0[part], outer_0[part])
        split_inverse(part, y_pair, 0, cuts[part])
        split_inverse(part, y_outer, cuts[part], rows_local)

    def split_rest(part):
        got(pair_1[part], outer_1[part])
        split_inverse(part, y_pair, cuts[part], rows_local)
        split_inverse(part, y_outer, 0, cuts[part])

    def split_far(part):
        got(far_0[part], far_1[part])
        split_inverse(part, y_far)

    def to_far_by_pair(part):
        got(pair_0[part])
        far_0[part] = relay_inverse(part, 0, y_pair, to_outer)

    def to_far_by_outer(part):
        got(outer_0[part])
        far_1[part] = relay_inverse(part, 1, y_outer, to_pair)

    def product(piece, group, entry, slot, outputs):
        block = lax.rem(pattern[(group * 2 + core) * 2 + entry, slot], rows_local)
        high, low = split(piece.T)
        for column, rows, part, total, at in outputs:
            at_inverse = (column * 2 + group, block, slice(None), columns(part))
            from_high, from_low = inv_high[at_inverse], inv_low[at_inverse]
            value = jnp.dot(high[:rows], from_high, preferred_element_type=jnp.float32)
            value += jnp.dot(low[:rows], from_high, preferred_element_type=jnp.float32)
            value += jnp.dot(high[:rows], from_low, preferred_element_type=jnp.float32)
            if group == 0 and entry == 0:
                total[at] = value
            else:
                total[at] += value

    def multiply(x_at, z_at, total, step, part):
        slot = z_at * (AXIS * AXIS) + x_at * AXIS + y
        for group in range(2):
            for entry in range(2):
                outputs = [
                    ((y_hi + side) % 2, height(step, side), part, total, place(step, side, part)) for side in range(2)
                ]
                product(pan[x_at, z_at, group, entry], group, entry, slot, outputs)

    def places(step):
        return turn(x, (0, 1, -1, 2)[step // 2]), (y_lo + 1 + step % 2) % 2

    def stays(step, side):
        return step % 2 == 1 and side == 0

    def height(step, side):
        return tile // 2 if step % 2 == 1 and side == 1 else tile

    def place(step, side, part):
        return step, side, slice(0, height(step, side)), columns(part)

    def cell(ref, step, side, part):
        first, width = (0, tile) if part is None else (part * lanes, lanes)
        return ref.at[step, side, pl.ds(0, height(step, side)), pl.ds(first, width)]

    def across(step, side, part):
        return pltpu.make_async_remote_copy(
            src_ref=cell(give, step, side, part), dst_ref=cell(take, step, side, part),
            send_sem=core_send.at[step, side, part or 0], recv_sem=core_recv.at[step, side, part or 0],
            device_id=sibling, device_id_type=MESH,
        )

    def first_row(x_at, y_at):
        return pl.multiple_of((x_at * AXIS + y_at) * tile, tile)

    def out_cell(x_at, y_at, rows, part):
        first, width = (0, tile) if part is None else (part * lanes, lanes)
        return out.at[pl.ds(first_row(x_at, y_at), rows), pl.ds(first, width)]

    def deliver(step, side, part):
        x_at, owner_lo = places(step)
        return pltpu.make_async_remote_copy(
            src_ref=cell(mine, step, side, part), dst_ref=out_cell(x_at, y, height(step, side), part),
            send_sem=out_send.at[step, side, part or 0], recv_sem=out_recv.at[y, x_at, part or 0],
            device_id=device(x, (y_hi + side) % 2 * 2 + owner_lo, z, core), device_id_type=MESH,
        )

    def factor_of(slot):
        return -active[slot].astype(jnp.float32)

    def finish(step, part):
        x_at, owner_lo = places(step)
        factor = factor_of((owner_lo * 2 + core) * (AXIS * AXIS) + x_at * AXIS + y)
        for side in (1, 0):
            across(step, side, part).wait_recv()
            at = place(step, side, part)
            value = (mine[at] + take[at]) * factor
            if stays(step, side):
                out[pl.ds(first_row(x_at, y), tile), columns(part)] = value
            else:
                mine[at] = value
                deliver(step, side, part).start()

    done = []
    pending = []

    def flush():
        while pending:
            pending.pop()()

    def unit(step, part=None):
        x_at, owner_lo = places(step)
        by = (0, 1, -1, 2)[step // 2]
        arrived(near, by)
        arrived(pair, by)
        multiply(x_at, owner_lo * 2 + 1 - core, give, step, part)
        for side in (1, 0):
            across(step, side, part).start()
        flush()
        multiply(x_at, owner_lo * 2 + core, mine, step, part)
        done.append((step, part))
        pending.append(functools.partial(finish, step, part))

    def far_multiply(x_at, z_at, total, number):
        slot = z_at * (AXIS * AXIS) + x_at * AXIS + y_far
        for group in range(2):
            for entry in range(2):
                piece = far_pan[x_at, (1 - group) * 2 + z_at % 2, entry]
                product(piece, group, entry, slot, [(y_hi, tile // 2, None, total, number)])

    def far_across(number):
        return pltpu.make_async_remote_copy(
            src_ref=far_give.at[number], dst_ref=far_take.at[number],
            send_sem=far_send.at[number], recv_sem=far_recv.at[number],
            device_id=sibling, device_id_type=MESH,
        )

    def far_unit(number):
        x_at, _ = places(2 * number)
        arrived(far, (0, 1, -1, 2)[number])
        far_multiply(x_at, y_lo * 2 + 1 - core, far_give, number)
        far_across(number).start()
        flush()
        far_multiply(x_at, y_lo * 2 + core, far_mine, number)
        pending.append(functools.partial(far_finish, number))

    def far_finish(number):
        x_at, _ = places(2 * number)
        factor = factor_of((y_lo * 2 + core) * (AXIS * AXIS) + x_at * AXIS + y_far)
        far_across(number).wait_recv()
        rows = pl.ds(first_row(x_at, y_far) + tile // 2, tile // 2)
        out[rows, :] = (far_mine[number] + far_take[number]) * factor

    outer_0[0] = give_own(0, 1, to_outer)
    swap = push("pan", panels_in.at[other], pan.at[x, z, y_lo], to_pair)
    outer_1[1] = give_own(1, 0, to_outer)
    near[1].start(panels_in.at[y_lo, 1])
    near[0].start(panels_in.at[y_lo, 0])
    split_own()
    near[0].turn_off(0, panels_in.at[y_lo, 0])
    near[1].turn_off(0, panels_in.at[y_lo, 1])
    near[1].turn_off(-1)
    near[1].on()
    near[0].turn_off(-1)
    pair_0[0] = give_own(0, 0, to_pair)
    outer_1[0] = give_own(0, 0, to_outer)
    near[0].on_again(0)
    got(swap)
    pair[1].start()
    pair_1[1] = give_own(1, 1, to_pair)
    got(swap)
    pair[0].start()
    near[1].turn_off(2)
    near[1].on_again(0)
    near[0].turn_off(1)
    pair[0].turn_off(1)
    got(swap, *near[0].beyond[0], *near[1].beyond["first"])
    crossing = push(
        "pan", pan.at[x, y_lo * 2 + z % 2, 1 - z // 2, :, :, pl.ds(tile // 2, tile // 2)], far_pan.at[x, z], to_far
    )
    got(swap)
    pair[1].turn_off(0)
    pair[1].on()
    pair_0[1] = give_own(1, 0, to_pair)
    got(swap)
    pair[0].turn_off(0)
    pair[1].turn_off(-1)
    pair[1].turn_off(1)
    to_far_by_pair(0)
    pair[1].turn_off(2)
    near[0].on_again(-1)
    pair_1[0] = give_own(0, 1, to_pair)
    pair[0].on()
    split_next(0)
    near[1].turn_off(1)
    pair[0].turn_off(-1)
    outer_0[1] = give_own(1, 1, to_outer)
    to_far_by_outer(0)
    got(crossing)
    far[1].start()
    pair[0].on_again(0)
    near[0].on_again(1)
    split_rest(1)
    pair[0].turn_off(2)
    got(crossing)
    far[0].start()
    to_far_by_pair(1)
    near[0].on()
    pair[1].on_again(0)
    got(crossing)
    far[1].turn_off(0)
    to_far_by_outer(1)
    pair[0].on_again(-1)
    pair[0].on_again(1)
    split_next(1)
    split_rest(0)
    pair[1].on_again(2)
    far[1].on()
    split_far(0)
    near[1].on_again(1)
    unit(0, 0)
    unit(1, 0)
    flush()
    near[0].turn_off(2)
    far[0].on()
    pair[1].on_again(-1)
    split_far(1)
    near[1].on_again(2)
    unit(0, 1)
    flush()
    pair[0].on_again(2)
    unit(2)
    flush()
    near[1].on_again(-1)
    far[1].turn_off(-1)
    got(crossing)
    far[0].turn_off(0)
    pair[1].on_again(1)
    far[0].turn_off(-1)
    unit(3)
    unit(1, 1)
    unit(4)
    flush()
    near[0].on_again(2)
    unit(5)
    flush()
    far[0].turn_off(1)
    far[1].turn_off(2)
    far[1].on_again(-1)
    far[0].turn_off(2)
    far[1].turn_off(1)
    far[0].on_again(-1)
    unit(6)
    flush()
    far[0].on_again(1)
    far[0].on_again(0)
    far[1].on_again(2)
    far[1].on_again(0)
    unit(7)
    flush()
    far[1].on_again(1)
    far[0].on_again(2)
    far_unit(2)
    far_unit(1)
    far_unit(0)
    far_unit(3)
    for _, copy in sent:
        got(copy)
        copy.wait_send()
    flush()
    for number in range(AXIS):
        far_across(number).wait_send()
    for step, part in done:
        for side in (1, 0):
            across(step, side, part).wait_send()
            if not stays(step, side):
                deliver(step, side, part).wait_send()
    for y_at in (y_pair, y_outer, y_far):
        rows = tile // 2 if y_at is y_far else tile
        for by in range(AXIS):
            x_at = turn(x, by)
            for part in (0, 1) if by == 0 else (None,):
                first, width = (0, tile) if part is None else (part * lanes, lanes)
                pltpu.make_async_remote_copy(
                    src_ref=mine.at[0, 0, pl.ds(0, rows), pl.ds(first, width)],
                    dst_ref=out_cell(x_at, y_at, rows, part),
                    send_sem=out_send.at[0, 0, 0], recv_sem=out_recv.at[y_at, x_at, part or 0],
                    device_id=to_pair, device_id_type=MESH,
                ).wait_recv()


def on_device(inverse_block, panels, pattern, active):
    rows, tile = inverse_block.shape
    rows_local = rows // tile
    per_group = panels.shape[1] // tile
    steps = AXIS * AXIS // 2
    dma = pltpu.SemaphoreType.DMA
    return pl.pallas_call(
        kernel,
        out_shape=pltpu.VMEM((AXIS * AXIS * tile, tile), jnp.float32),
        in_specs=[pl.BlockSpec(memory_space=pl.ANY)] * 2 + [pl.BlockSpec(memory_space=pltpu.SMEM)] * 2,
        out_specs=pl.BlockSpec(memory_space=pltpu.VMEM),
        scratch_shapes=[
            pltpu.VMEM((2, AXIS, rows_local, tile, tile // 2), jnp.float32),
            pltpu.VMEM((AXIS, rows_local, tile, tile), jnp.bfloat16),
            pltpu.VMEM((AXIS, rows_local, tile, tile), jnp.bfloat16),
            pltpu.VMEM((AXIS, AXIS, 2, per_group, tile, tile), jnp.float32),
            pltpu.VMEM((AXIS, AXIS, per_group, tile, tile // 2), jnp.float32),
            pltpu.VMEM((steps, 2, tile, tile), jnp.float32),
            pltpu.VMEM((steps, 2, tile, tile), jnp.float32),
            pltpu.VMEM((steps, 2, tile, tile), jnp.float32),
            pltpu.VMEM((AXIS, tile // 2, tile), jnp.float32),
            pltpu.VMEM((AXIS, tile // 2, tile), jnp.float32),
            pltpu.VMEM((AXIS, tile // 2, tile), jnp.float32),
            dma((3,)),
            dma((12,)), dma((12,)),
            dma((122,)), dma((122,)),
            dma((steps, 2, 2)), dma((steps, 2, 2)),
            dma((AXIS,)), dma((AXIS,)),
            dma((steps, 2, 2)), dma((AXIS, AXIS, 2)),
        ],
        compiler_params=pltpu.CompilerParams(
            collective_id=0, has_side_effects=True, vmem_limit_bytes=56 * 1024 * 1024
        ),
        cost_estimate=pl.CostEstimate(flops=6 * 128 * tile**3, bytes_accessed=20 * 1024 * 1024, transcendentals=0),
        name="selected_inverse",
    )(
        inverse_block.reshape(rows_local, tile, tile),
        panels.reshape(panels.shape[0], per_group, tile, tile),
        pattern.T,
        active,
    )


def solution(mesh):
    in_specs = (P("row", "col"), P("col", "row", None), P(), P())
    out_specs = P("row", "col")
    return jax.shard_map(
        on_device, mesh=mesh, in_specs=in_specs, out_specs=out_specs, check_vma=False
    )
```

```python
import functools

import jax
import jax.numpy as jnp
from jax import lax
from jax.experimental import pallas as pl
from jax.experimental.pallas import tpu as pltpu
from jax.sharding import PartitionSpec as P

MESH = pl.DeviceIdType.MESH
AXIS = 4


def split(value):
    high = value.astype(jnp.bfloat16)
    low = (value - high.astype(jnp.float32)).astype(jnp.bfloat16)
    return high, low


def kernel(
    inverse_in, panels_in, pattern, active, out,
    inverse, inv_high, inv_low, pan, far_pan, give, take, mine, far_give, far_take, far_mine,
    own_sem, inv_send, inv_recv, pan_send, pan_recv, core_send, core_recv, far_send, far_recv, out_send, out_recv,
):
    tile = panels_in.shape[3]
    rows_local = inverse_in.shape[0]

    col, row = lax.axis_index("col"), lax.axis_index("row")
    z, x, y_hi = col // (2 * AXIS), col // 2 % AXIS, col % 2
    y_lo, core = row // 2, row % 2
    y = y_hi * 2 + y_lo

    def device(x_at, y_at, z_at, core_at):
        return (z_at * 2 * AXIS + x_at * 2 + y_at // 2, y_at % 2 * 2 + core_at)

    def turn(at, by):
        return (at + by + AXIS) % AXIS

    def along(axis, by):
        if axis == "x":
            return device(turn(x, by), y, z, core)
        if axis == "y":
            return device(x, turn(y, by), z, core)
        return device(x, y, turn(z, by), core)

    y_pair, y_outer, y_far = y_hi * 2 + 1 - y_lo, (1 - y_hi) * 2 + 1 - y_lo, (1 - y_hi) * 2 + y_lo
    to_pair, to_outer, to_far = (device(x, y_at, z, core) for y_at in (y_pair, y_outer, y_far))
    sibling = device(x, y, z, 1 - core)

    barrier = pltpu.get_barrier_semaphore()
    peers = [along("x", 1), along("x", -1), along("z", 1), along("z", -1)]
    peers += [to_pair, to_outer, to_far, sibling]
    for peer in peers:
        pl.semaphore_signal(barrier, inc=1, device_id=peer, device_id_type=MESH)
    pl.semaphore_wait(barrier, len(peers))

    sent = []

    def push(kind, source, target, to):
        sends, receives = (inv_send, inv_recv) if kind == "inv" else (pan_send, pan_recv)
        number = len([entry for entry in sent if entry[0] == kind])
        copy = pltpu.make_async_remote_copy(
            src_ref=source, dst_ref=target, send_sem=sends.at[number], recv_sem=receives.at[number],
            device_id=to, device_id_type=MESH,
        )
        copy.start()
        sent.append((kind, copy))
        return copy

    received = []

    def got(*copies):
        for copy in copies:
            if not any(copy is known for known in received):
                copy.wait_recv()
                received.append(copy)

    class Way:
        def __init__(self, hold, first, second):
            self.hold, self.first, self.second = hold, first, second
            self.next_to, self.beyond = {}, {}

        def view(self, by_first, by_second, half=None):
            by_x, by_z = (by_first, by_second) if self.first == "x" else (by_second, by_first)
            tile_at = self.hold(turn(x, by_x), turn(z, by_z))
            return tile_at if half is None else tile_at.at[pl.ds(half * (tile // 2), tile // 2)]

        def spread(self, key, axis, at, source=None):
            source = self.view(*at) if source is None else source
            self.next_to[key] = [push("pan", source, self.view(*at), along(axis, by)) for by in (1, -1)]

        def relay(self, key, axis, at_below, at_above):
            up, down = self.next_to[key]
            got(up)
            below = self.view(*at_below, half=0)
            far_up = push("pan", below, below, along(axis, 1))
            got(down)
            above = self.view(*at_above, half=1)
            self.beyond[key] = [far_up, push("pan", above, above, along(axis, -1))]

        def start(self, source=None):
            self.spread("first", self.first, (0, 0), source)

        def on(self):
            self.relay("first", self.first, (-1, 0), (1, 0))

        def turn_off(self, by, source=None):
            if by == 2:
                got(*self.beyond["first"])
            elif by != 0:
                got(*self.next_to["first"])
            self.spread(by, self.second, (by, 0), source)

        def on_again(self, by):
            self.relay(by, self.second, (by, -1), (by, 1))

    other = 1 - y_lo
    near = [Way(lambda *at: pan.at[*at, y_lo, 0], "x", "z"), Way(lambda *at: pan.at[*at, y_lo, 1], "z", "x")]
    pair = [Way(lambda *at: pan.at[*at, other, 0], "x", "z"), Way(lambda *at: pan.at[*at, other, 1], "z", "x")]
    far = [Way(lambda *at: far_pan.at[*at, 0], "x", "z"), Way(lambda *at: far_pan.at[*at, 1], "z", "x")]

    def arrived(ways, by):
        along_x, along_z = ways
        got(*along_x.beyond[by])
        if by == 0:
            got(*along_z.beyond["first"])
        else:
            for at in (0, -1, 1, 2):
                got(*(along_z.beyond if by == 2 else along_z.next_to)[at])

    lanes = tile // 2
    cuts = (rows_local * 4 // 8, rows_local * 6 // 8)

    def span_of(part, span):
        return (pl.ds(0, cuts[part]), pl.ds(cuts[part], rows_local - cuts[part]))[span]

    def columns(part):
        return slice(None) if part is None else slice(part * lanes, (part + 1) * lanes)

    def own(part, span):
        return inverse_in.at[span_of(part, span), :, pl.ds(part * lanes, lanes)]

    def held(part, y_at, span):
        return inverse.at[part, y_at, span_of(part, span)]

    def give_own(part, span, to):
        return push("inv", own(part, span), held(part, y, span), to)

    def relay_inverse(part, span, y_at, to):
        return push("inv", held(part, y_at, span), held(part, y_at, span), to)

    pair_0, outer_0, pair_1, outer_1, far_0, far_1 = ([None, None] for _ in range(6))
    own_copies = [
        pltpu.make_async_copy(inverse_in.at[:, :, pl.ds(part * lanes, lanes)], inverse.at[part, y], own_sem.at[part])
        for part in range(2)
    ]
    own_copies.append(pltpu.make_async_copy(panels_in.at[y_lo], pan.at[x, z, y_lo], own_sem.at[2]))
    def split_inverse(part, y_at, first=0, last=rows_local):
        def body(block):
            high, low = split(inverse[part, y_at, block])
            inv_high[y_at, block, :, columns(part)] = high
            inv_low[y_at, block, :, columns(part)] = low

        pl.loop(first, last)(body)

    def split_own():
        for copy in own_copies:
            copy.start()
        for copy in own_copies:
            copy.wait()
        split_inverse(0, y)
        split_inverse(1, y)

    def split_next(part):
        got(pair_0[part], outer_0[part])
        split_inverse(part, y_pair, 0, cuts[part])
        split_inverse(part, y_outer, cuts[part], rows_local)

    def split_rest(part):
        got(pair_1[part], outer_1[part])
        split_inverse(part, y_pair, cuts[part], rows_local)
        split_inverse(part, y_outer, 0, cuts[part])

    def split_far(part):
        got(far_0[part], far_1[part])
        split_inverse(part, y_far)

    def to_far_by_pair(part):
        got(pair_0[part])
        far_0[part] = relay_inverse(part, 0, y_pair, to_outer)

    def to_far_by_outer(part):
        got(outer_0[part])
        far_1[part] = relay_inverse(part, 1, y_outer, to_pair)

    def product(piece, group, entry, slot, outputs):
        block = lax.rem(pattern[(group * 2 + core) * 2 + entry, slot], rows_local)
        high, low = split(piece.T)
        for column, rows, part, total, at in outputs:
            at_inverse = (column * 2 + group, block, slice(None), columns(part))
            from_high, from_low = inv_high[at_inverse], inv_low[at_inverse]
            value = jnp.dot(high[:rows], from_high, preferred_element_type=jnp.float32)
            value += jnp.dot(low[:rows], from_high, preferred_element_type=jnp.float32)
            value += jnp.dot(high[:rows], from_low, preferred_element_type=jnp.float32)
            if group == 0 and entry == 0:
                total[at] = value
            else:
                total[at] += value

    def multiply(x_at, z_at, total, step, part):
        slot = z_at * (AXIS * AXIS) + x_at * AXIS + y
        for group in range(2):
            for entry in range(2):
                outputs = [
                    ((y_hi + side) % 2, height(step, side), part, total, place(step, side, part)) for side in range(2)
                ]
                product(pan[x_at, z_at, group, entry], group, entry, slot, outputs)

    def places(step):
        return turn(x, (0, 1, -1, 2)[step // 2]), (y_lo + 1 + step % 2) % 2

    def stays(step, side):
        return step % 2 == 1 and side == 0

    def height(step, side):
        return tile // 2 if step % 2 == 1 and side == 1 else tile

    def place(step, side, part):
        return step, side, slice(0, height(step, side)), columns(part)

    def cell(ref, step, side, part):
        first, width = (0, tile) if part is None else (part * lanes, lanes)
        return ref.at[step, side, pl.ds(0, height(step, side)), pl.ds(first, width)]

    def across(step, side, part):
        return pltpu.make_async_remote_copy(
            src_ref=cell(give, step, side, part), dst_ref=cell(take, step, side, part),
            send_sem=core_send.at[step, side, part or 0], recv_sem=core_recv.at[step, side, part or 0],
            device_id=sibling, device_id_type=MESH,
        )

    def first_row(x_at, y_at):
        return pl.multiple_of((x_at * AXIS + y_at) * tile, tile)

    def out_cell(x_at, y_at, rows, part):
        first, width = (0, tile) if part is None else (part * lanes, lanes)
        return out.at[pl.ds(first_row(x_at, y_at), rows), pl.ds(first, width)]

    def deliver(step, side, part):
        x_at, owner_lo = places(step)
        return pltpu.make_async_remote_copy(
            src_ref=cell(mine, step, side, part), dst_ref=out_cell(x_at, y, height(step, side), part),
            send_sem=out_send.at[step, side, part or 0], recv_sem=out_recv.at[y, x_at, part or 0],
            device_id=device(x, (y_hi + side) % 2 * 2 + owner_lo, z, core), device_id_type=MESH,
        )

    def factor_of(slot):
        return -active[slot].astype(jnp.float32)

    def finish(step, part):
        x_at, owner_lo = places(step)
        factor = factor_of((owner_lo * 2 + core) * (AXIS * AXIS) + x_at * AXIS + y)
        for side in (1, 0):
            across(step, side, part).wait_recv()
            at = place(step, side, part)
            value = (mine[at] + take[at]) * factor
            if stays(step, side):
                out[pl.ds(first_row(x_at, y), tile), columns(part)] = value
            else:
                mine[at] = value
                deliver(step, side, part).start()

    done = []
    pending = []

    def flush():
        while pending:
            pending.pop()()

    def unit(step, part=None):
        x_at, owner_lo = places(step)
        by = (0, 1, -1, 2)[step // 2]
        arrived(near, by)
        arrived(pair, by)
        multiply(x_at, owner_lo * 2 + 1 - core, give, step, part)
        for side in (1, 0):
            across(step, side, part).start()
        flush()
        multiply(x_at, owner_lo * 2 + core, mine, step, part)
        done.append((step, part))
        pending.append(functools.partial(finish, step, part))

    def far_multiply(x_at, z_at, total, number):
        slot = z_at * (AXIS * AXIS) + x_at * AXIS + y_far
        for group in range(2):
            for entry in range(2):
                piece = far_pan[x_at, (1 - group) * 2 + z_at % 2, entry]
                product(piece, group, entry, slot, [(y_hi, tile // 2, None, total, number)])

    def far_across(number):
        return pltpu.make_async_remote_copy(
            src_ref=far_give.at[number], dst_ref=far_take.at[number],
            send_sem=far_send.at[number], recv_sem=far_recv.at[number],
            device_id=sibling, device_id_type=MESH,
        )

    def far_unit(number):
        x_at, _ = places(2 * number)
        arrived(far, (0, 1, -1, 2)[number])
        far_multiply(x_at, y_lo * 2 + 1 - core, far_give, number)
        far_across(number).start()
        flush()
        far_multiply(x_at, y_lo * 2 + core, far_mine, number)
        pending.append(functools.partial(far_finish, number))

    def far_finish(number):
        x_at, _ = places(2 * number)
        factor = factor_of((y_lo * 2 + core) * (AXIS * AXIS) + x_at * AXIS + y_far)
        far_across(number).wait_recv()
        rows = pl.ds(first_row(x_at, y_far) + tile // 2, tile // 2)
        out[rows, :] = (far_mine[number] + far_take[number]) * factor

    outer_0[0] = give_own(0, 1, to_outer)
    swap = push("pan", panels_in.at[other], pan.at[x, z, y_lo], to_pair)
    outer_1[1] = give_own(1, 0, to_outer)
    near[1].start(panels_in.at[y_lo, 1])
    near[0].start(panels_in.at[y_lo, 0])
    near[0].turn_off(0, panels_in.at[y_lo, 0])
    near[1].turn_off(0, panels_in.at[y_lo, 1])
    split_own()
    near[1].turn_off(-1)
    near[1].on()
    near[0].turn_off(-1)
    pair_0[0] = give_own(0, 0, to_pair)
    outer_1[0] = give_own(0, 0, to_outer)
    near[0].on_again(0)
    got(swap)
    pair[1].start()
    pair_1[1] = give_own(1, 1, to_pair)
    got(swap)
    pair[0].start()
    near[1].turn_off(2)
    near[1].on_again(0)
    near[0].turn_off(1)
    pair[0].turn_off(1)
    got(swap, *near[0].beyond[0], *near[1].beyond["first"])
    crossing = push(
        "pan", pan.at[x, y_lo * 2 + z % 2, 1 - z // 2, :, :, pl.ds(tile // 2, tile // 2)], far_pan.at[x, z], to_far
    )
    got(swap)
    pair[1].turn_off(0)
    pair[1].on()
    pair_0[1] = give_own(1, 0, to_pair)
    got(swap)
    pair[0].turn_off(0)
    pair[1].turn_off(-1)
    pair[1].turn_off(1)
    to_far_by_pair(0)
    pair[1].turn_off(2)
    near[0].on_again(-1)
    pair_1[0] = give_own(0, 1, to_pair)
    pair[0].on()
    split_next(0)
    near[1].turn_off(1)
    pair[0].turn_off(-1)
    outer_0[1] = give_own(1, 1, to_outer)
    to_far_by_outer(0)
    got(crossing)
    far[1].start()
    pair[0].on_again(0)
    near[0].on_again(1)
    split_rest(1)
    pair[0].turn_off(2)
    got(crossing)
    far[0].start()
    to_far_by_pair(1)
    near[0].on()
    pair[1].on_again(0)
    got(crossing)
    far[1].turn_off(0)
    to_far_by_outer(1)
    pair[0].on_again(-1)
    pair[0].on_again(1)
    split_next(1)
    split_rest(0)
    pair[1].on_again(2)
    far[1].on()
    split_far(0)
    near[1].on_again(1)
    unit(0, 0)
    unit(1, 0)
    flush()
    near[0].turn_off(2)
    far[0].on()
    pair[1].on_again(-1)
    split_far(1)
    near[1].on_again(2)
    unit(0, 1)
    flush()
    pair[0].on_again(2)
    unit(2)
    flush()
    near[1].on_again(-1)
    far[1].turn_off(-1)
    got(crossing)
    far[0].turn_off(0)
    pair[1].on_again(1)
    far[0].turn_off(-1)
    unit(3)
    unit(1, 1)
    unit(4)
    flush()
    near[0].on_again(2)
    unit(5)
    flush()
    far[0].turn_off(1)
    far[1].turn_off(2)
    far[1].on_again(-1)
    far[0].turn_off(2)
    far[1].turn_off(1)
    far[0].on_again(-1)
    unit(6)
    flush()
    far[0].on_again(1)
    far[0].on_again(0)
    far[1].on_again(2)
    far[1].on_again(0)
    unit(7)
    flush()
    far[1].on_again(1)
    far[0].on_again(2)
    far_unit(2)
    far_unit(1)
    far_unit(0)
    far_unit(3)
    for _, copy in sent:
        got(copy)
        copy.wait_send()
    flush()
    for number in range(AXIS):
        far_across(number).wait_send()
    for step, part in done:
        for side in (1, 0):
            across(step, side, part).wait_send()
            if not stays(step, side):
                deliver(step, side, part).wait_send()
    for y_at in (y_pair, y_outer, y_far):
        rows = tile // 2 if y_at is y_far else tile
        for by in range(AXIS):
            x_at = turn(x, by)
            for part in (0, 1) if by == 0 else (None,):
                first, width = (0, tile) if part is None else (part * lanes, lanes)
                pltpu.make_async_remote_copy(
                    src_ref=mine.at[0, 0, pl.ds(0, rows), pl.ds(first, width)],
                    dst_ref=out_cell(x_at, y_at, rows, part),
                    send_sem=out_send.at[0, 0, 0], recv_sem=out_recv.at[y_at, x_at, part or 0],
                    device_id=to_pair, device_id_type=MESH,
                ).wait_recv()


def on_device(inverse_block, panels, pattern, active):
    rows, tile = inverse_block.shape
    rows_local = rows // tile
    per_group = panels.shape[1] // tile
    steps = AXIS * AXIS // 2
    dma = pltpu.SemaphoreType.DMA
    return pl.pallas_call(
        kernel,
        out_shape=pltpu.VMEM((AXIS * AXIS * tile, tile), jnp.float32),
        in_specs=[pl.BlockSpec(memory_space=pl.ANY)] * 2 + [pl.BlockSpec(memory_space=pltpu.SMEM)] * 2,
        out_specs=pl.BlockSpec(memory_space=pltpu.VMEM),
        scratch_shapes=[
            pltpu.VMEM((2, AXIS, rows_local, tile, tile // 2), jnp.float32),
            pltpu.VMEM((AXIS, rows_local, tile, tile), jnp.bfloat16),
            pltpu.VMEM((AXIS, rows_local, tile, tile), jnp.bfloat16),
            pltpu.VMEM((AXIS, AXIS, 2, per_group, tile, tile), jnp.float32),
            pltpu.VMEM((AXIS, AXIS, per_group, tile, tile // 2), jnp.float32),
            pltpu.VMEM((steps, 2, tile, tile), jnp.float32),
            pltpu.VMEM((steps, 2, tile, tile), jnp.float32),
            pltpu.VMEM((steps, 2, tile, tile), jnp.float32),
            pltpu.VMEM((AXIS, tile // 2, tile), jnp.float32),
            pltpu.VMEM((AXIS, tile // 2, tile), jnp.float32),
            pltpu.VMEM((AXIS, tile // 2, tile), jnp.float32),
            dma((3,)),
            dma((12,)), dma((12,)),
            dma((122,)), dma((122,)),
            dma((steps, 2, 2)), dma((steps, 2, 2)),
            dma((AXIS,)), dma((AXIS,)),
            dma((steps, 2, 2)), dma((AXIS, AXIS, 2)),
        ],
        compiler_params=pltpu.CompilerParams(
            collective_id=0, has_side_effects=True, vmem_limit_bytes=56 * 1024 * 1024
        ),
        cost_estimate=pl.CostEstimate(flops=6 * 128 * tile**3, bytes_accessed=20 * 1024 * 1024, transcendentals=0),
        name="selected_inverse",
    )(
        inverse_block.reshape(rows_local, tile, tile),
        panels.reshape(panels.shape[0], per_group, tile, tile),
        pattern.T,
        active,
    )


def solution(mesh):
    in_specs = (P("row", "col"), P("col", "row", None), P(), P())
    out_specs = P("row", "col")
    return jax.shard_map(
        on_device, mesh=mesh, in_specs=in_specs, out_specs=out_specs, check_vma=False
    )
```
